32 devices in a mesh: gx: 8 (over z, y), gy: 4 (over x, core).
Axes of the slice: x: 2, y: 2, z: 4, core: 2. Of those that a mesh axis runs over, the one named last changes fastest.
Arguments:
- positions: float32 [3, 1024], P(None, ('gx', 'gy')), may hold values from -4 to 4
- species: int32 [1024], P(('gx', 'gy')), may hold values from 0 to 7
- atom_count: int32 [32], P(('gx', 'gy')), may hold values from 10 to 32, as said below
- send_list: int32 [32, 8, 4], P(('gx', 'gy')), may hold values from 0 to 31, as said below
- edges: int32 [32, 2, 256], P(('gx', 'gy')), may hold values from 0 to 63, as said below
- centre_embed: float32 [512, 8], replicated, may hold values from -3 to 3
- neighbour_embed: float32 [512, 8], replicated, may hold values from -3 to 3
- radial_weight: float32 [512, 8], replicated, may hold values from -2 to 2
- env_weight: float32 [2, 64, 512], replicated, may hold values from -0.25 to 0.25
- latent_weight: float32 [2, 512, 704], replicated, may hold values from -0.21875 to 0.21875
- out_weight: float32 [512, 512], replicated, may hold values from -0.25 to 0.25
- head_weight: float32 [2, 512], replicated, may hold values from -0.25 to 0.25
Outputs:
- atom_energy: float32 [1024], P(('gx', 'gy'))
- forces: float32 [3, 1024], P(None, ('gx', 'gy'))
The draws below stay inside these ranges and needn't reach their ends.
Inputs may be any that keep to these rules, and one draw needn't show every extreme that they name: Device p's live atoms are its slots 0 to atom_count[p] - 1, the rest are padding; its live edges are its first 8 atom_count[p] edge slots. send_list[p, k, g] is a live atom of device p; the 4 atoms of one (p, k) are distinct and are sent to the device at offset k. `edges`: row 0 is a live atom slot of the device; row 1 is a live atom slot other than the centre, or a ghost slot 32 + k * 4 + g.
All inputs are finite; a program needn't handle non-finite values.
Results may differ from the reference program's by a relative error of at most 0.00025.
Values sent between devices are 32-bit elements; how exact they have to be, the bound alone decides.
No kernel may reach another device: no remote copies, remote signals or barrier semaphores. Data moves between devices by JAX's collectives and lax.ppermute only.
A program may use at most 64 MiB of HBM per device.

```python
import math
import jax
import jax.numpy as jnp
from jax import lax

TENSOR = 64
LATENT = 512
HARM = 9
BASIS = 8
SPECIES = 8
LAYERS = 2
ATOM_DEV = 32
GHOST = 4
EDGES = 256
ATOMS = 1024
N_GX = 8
N_GY = 4


def count_draw(key):
    key = jax.random.fold_in(key, 101)
    devices = ATOMS // ATOM_DEV
    lowest = ATOM_DEV // 3
    key_level, key_full, key_low = jax.random.split(key, 3)
    level = jax.random.randint(key_level, (devices,), 0, 33)
    counts = lowest + (ATOM_DEV - lowest) * level * level * level // 32768
    full_at = jax.random.randint(key_full, (), 0, devices)
    low_at = (full_at + 1 + jax.random.randint(key_low, (), 0, devices - 1)) % devices
    counts = counts.at[full_at].set(ATOM_DEV)
    counts = counts.at[low_at].set(lowest)
    return counts.astype(jnp.int32)


def draw_atom_count(key, part):
    counts = count_draw(key)
    return counts


def draw_send_list(key, part):
    counts = count_draw(key)
    key = jax.random.fold_in(key, 7)
    devices = ATOMS // ATOM_DEV
    place = jnp.arange(ATOM_DEV, dtype=jnp.int32)[None, None, :]
    scores = jax.random.randint(key, (devices, 8, ATOM_DEV), 0, 2 ** 19) * ATOM_DEV + place
    limit = counts[:, None, None]
    scores = jnp.where(place == limit - 1, 2 ** 30, scores)
    scores = jnp.where(place == 0, 2 ** 30 - 1, scores)
    scores = jnp.where(place >= limit, -1, scores)
    _, chosen = lax.top_k(scores, GHOST)
    return chosen.astype(jnp.int32)


def draw_edges(key, part):
    counts = count_draw(key)
    key = jax.random.fold_in(key, 13)
    devices = ATOMS // ATOM_DEV
    key_centre, key_step, key_ghost, key_pick = jax.random.split(key, 4)
    limit = counts[:, None]
    centre = jax.random.randint(key_centre, (devices, EDGES), 0, limit)
    centre = centre.at[:, 0].set(0)
    step = jax.random.randint(key_step, (devices, EDGES), 0, limit - 1)
    partner = (centre + 1 + step) % limit
    ghost = jax.random.randint(key_ghost, (devices, EDGES), 0, 8 * GHOST)
    pick = jax.random.randint(key_pick, (devices, EDGES), 0, 2)
    other = jnp.where(pick == 1, ATOM_DEV + ghost, partner)
    other = other.at[:, EDGES - 1].set(ATOM_DEV + 8 * GHOST - 1)
    return jnp.stack([centre, other], axis=1).astype(jnp.int32)


def with_ends(result, rng, smallest, largest):
    spot = [jax.random.randint(jax.random.fold_in(rng, axis), (), 0, length) for axis, length in enumerate(result.shape)]
    longest = result.shape.index(max(result.shape))
    beside = spot[:longest] + [(spot[longest] + 1) % result.shape[longest]] + spot[longest + 1:]
    return result.at[tuple(spot)].set(smallest).at[tuple(beside)].set(largest)


def level_of(own_key, extent, pieces, low, high):
    factor_of = 1.0
    for dim, shards_of in pieces:
        draws = jax.random.uniform(jax.random.fold_in(jax.random.fold_in(own_key, 6), dim), (shards_of,), jnp.float32, low / len(pieces), high / len(pieces))
        factor_of = factor_of * jnp.repeat(jnp.exp(draws), extent[dim] // shards_of).reshape((-1,) + (1,) * (len(extent) - 1 - dim))
    return factor_of


def normal_values(rng, shape, scale, most, cuts=(), held_as=jnp.bfloat16):
    factor_of = level_of(rng, shape, cuts, -0.22, 0.18) if cuts else 1.0
    values = jax.random.normal(rng, shape, jnp.float32) * scale * factor_of
    return jnp.minimum(jnp.maximum(values, -most), most).astype(held_as)


def setup_inputs(seed: int = 0) -> dict:
    key_of = jax.random.split(jax.random.key(seed), 13)
    return {
        "positions": normal_values(key_of[0], (3, ATOMS), 0.7, 4.0, ((1, 32),), jnp.float32),
        "species": with_ends(jax.random.randint(key_of[1], (ATOMS,), 0, SPECIES), jax.random.fold_in(key_of[1], 1), 0, SPECIES - 1).astype(jnp.int32),
        "atom_count": draw_atom_count(jax.random.fold_in(key_of[12], 71), 0),
        "send_list": draw_send_list(jax.random.fold_in(key_of[12], 71), 0),
        "edges": draw_edges(jax.random.fold_in(key_of[12], 71), 0),
        "centre_embed": normal_values(key_of[5], (LATENT, SPECIES), 0.5, 3.0, (), jnp.float32),
        "neighbour_embed": normal_values(key_of[6], (LATENT, SPECIES), 0.5, 3.0, (), jnp.float32),
        "radial_weight": normal_values(key_of[7], (LATENT, BASIS), BASIS ** -0.5, 2.0, (), jnp.float32),
        "env_weight": normal_values(key_of[8], (LAYERS, TENSOR, LATENT), LATENT ** -0.5, 0.25, (), jnp.float32),
        "latent_weight": normal_values(key_of[9], (LAYERS, LATENT, LATENT + 3 * TENSOR), (LATENT + 3 * TENSOR) ** -0.5, 0.21875, (), jnp.float32),
        "out_weight": normal_values(key_of[10], (LATENT, LATENT), LATENT ** -0.5, 0.25, (), jnp.float32),
        "head_weight": normal_values(key_of[11], (2, LATENT), LATENT ** -0.5, 0.25, (), jnp.float32),
    }


offset_x = (-1, -1, -1, 0, 0, 1, 1, 1)
offset_y = (-1, 0, 1, -1, 1, -1, 0, 1)
highest = lax.Precision.HIGHEST

def parity():
    return jnp.array([1.0, -1.0, -1.0, -1.0, 1.0, 1.0, 1.0, 1.0, 1.0], dtype=jnp.float32)

def harmonics(unit):
    root = math.sqrt(3.0)
    along_x, along_y, along_z = (unit[0], unit[1], unit[2])
    return jnp.stack([jnp.ones_like(along_x), along_x, along_y, along_z, root * along_x * along_y, root * along_y * along_z, 0.5 * (3.0 * along_z * along_z - 1.0), root * along_x * along_z, 0.5 * root * (along_x * along_x - along_y * along_y)])

def geometry(start, finish, count_basis):
    offset = finish - start
    squared = lax.optimization_barrier(jnp.sum(offset * offset, axis=0))
    unit = offset / jnp.sqrt(1.0 + squared)
    length = jnp.sqrt(squared)
    centres = 0.5 * jnp.arange(count_basis, dtype=jnp.float32)
    basis = jnp.exp(-2.0 * (length[None, :] - centres[:, None]) ** 2)
    return (unit, basis, harmonics(unit))

def refine(hidden, env_centre, env_other, harm, weight):
    sign = parity()[None, :, None]
    product = (env_centre + env_other * sign) * harm[None]
    scalars = jnp.concatenate([hidden, product[:, 0], lax.optimization_barrier(jnp.sum(product[:, 1:4], axis=1)), lax.optimization_barrier(jnp.sum(product[:, 4:9], axis=1))], axis=0)
    return hidden + jax.nn.silu(jnp.dot(weight, scalars, precision=highest))

def reference(positions, species, atom_count, send_list, edges, centre_embed, neighbour_embed, radial_weight, env_weight, latent_weight, out_weight, head_weight):
    devices = N_GX * N_GY
    place = jnp.arange(devices, dtype=jnp.int32)
    row_x = place // N_GY
    row_y = place % N_GY
    step_x = jnp.array(offset_x, dtype=jnp.int32)
    step_y = jnp.array(offset_y, dtype=jnp.int32)
    source = (row_x[:, None] + step_x[None, :]) % N_GX * N_GY + (row_y[:, None] + step_y[None, :]) % N_GY
    back = 7 - jnp.arange(8, dtype=jnp.int32)
    ghost_atom = source[:, :, None] * ATOM_DEV + send_list[source, back[None, :]]
    own_slots = place[:, None] * ATOM_DEV + jnp.arange(ATOM_DEV, dtype=jnp.int32)[None, :]
    slots = jnp.concatenate([own_slots, ghost_atom.reshape(devices, 8 * GHOST)], axis=1).astype(jnp.int32)
    centre = (place[:, None] * ATOM_DEV + edges[:, 0, :]).astype(jnp.int32)
    other = jnp.take_along_axis(slots, edges[:, 1, :].astype(jnp.int32), axis=1).astype(jnp.int32)
    per_atom = EDGES // ATOM_DEV
    live = (jnp.arange(EDGES, dtype=jnp.int32)[None, :] < per_atom * atom_count[:, None]).astype(jnp.float32)
    parity_rows = jnp.tile(parity(), TENSOR)[:, None]

    def initial(pair):
        centre_ids, other_ids = pair
        unit, basis, harm = geometry(positions[:, centre_ids], positions[:, other_ids], BASIS)
        inner = jnp.dot(radial_weight, basis, precision=highest)
        inner = inner + centre_embed[:, species[centre_ids]] + neighbour_embed[:, species[other_ids]]
        return jax.nn.silu(inner)
    hidden = lax.map(initial, (centre, other))
    for layer in range(LAYERS):

        def accumulate(env, inputs):
            block, centre_ids, other_ids, alive = inputs
            unit, basis, harm = geometry(positions[:, centre_ids], positions[:, other_ids], BASIS)
            weights_e = jnp.dot(env_weight[layer], block, precision=highest)
            contrib = (weights_e[:, None, :] * harm[None]).reshape(TENSOR * HARM, EDGES) * (alive * 0.25)
            env = env.at[:, centre_ids].add(contrib)
            env = env.at[:, other_ids].add(contrib * parity_rows)
            return (env, None)
        env, _ = lax.scan(accumulate, jnp.zeros((TENSOR * HARM, ATOMS), jnp.float32), (hidden, centre, other, live))

        def update(inputs):
            block, centre_ids, other_ids = inputs
            unit, basis, harm = geometry(positions[:, centre_ids], positions[:, other_ids], BASIS)
            env_centre = env[:, centre_ids].reshape(TENSOR, HARM, EDGES)
            env_other = env[:, other_ids].reshape(TENSOR, HARM, EDGES)
            return refine(block, env_centre, env_other, harm, latent_weight[layer])
        hidden = lax.map(update, (hidden, centre, other))

    def finish_sums(totals, inputs):
        block, centre_ids, other_ids, alive = inputs
        unit, basis, harm = geometry(positions[:, centre_ids], positions[:, other_ids], BASIS)
        latent = jax.nn.silu(jnp.dot(out_weight, block, precision=highest))
        heads = jnp.dot(head_weight, latent, precision=highest)
        energy_e = 0.5 * heads[0] * alive
        push = heads[1] * alive * unit
        totals = totals.at[:, centre_ids].add(jnp.concatenate([energy_e[None], push], axis=0))
        totals = totals.at[:, other_ids].add(jnp.concatenate([energy_e[None], -push], axis=0))
        return (totals, None)
    totals, _ = lax.scan(finish_sums, jnp.zeros((4, ATOMS), jnp.float32), (hidden, centre, other, live))
    return (totals[0], totals[1:4])
```

```python
import functools
import math

import jax
import jax.numpy as jnp
import numpy as np
from jax import lax
from jax.experimental import pallas as pl
from jax.experimental.pallas import tpu as pltpu
from jax.sharding import PartitionSpec as P

offset_x = (-1, -1, -1, 0, 0, 1, 1, 1)
offset_y = (-1, 0, 1, -1, 1, -1, 0, 1)
f32 = jnp.float32
bf16 = jnp.bfloat16
highest = lax.Precision.HIGHEST
order = (0, 4, 5, 6, 7, 8, 1, 2, 3)
even_count = 6
ATOMS = 32
LANES = 128


def folded(position, length):
    if length % 2:
        return position
    half = length // 2
    return 2 * position if position < half else 2 * (length - 1 - position) + 1


class Layout:
    def __init__(self, size_x, size_y):
        self.size_x, self.size_y = size_x, size_y
        self.count = size_x * size_y
        self.device = np.zeros((size_x, size_y), np.int32)
        self.domain = np.zeros((self.count, 2), np.int32)
        for x in range(size_x):
            for y in range(size_y):
                at = folded(x, size_x) * size_y + y
                self.device[x, y] = at
                self.domain[at] = (x, y)

    def home(self, x, y):
        return (x % self.size_x) * self.size_y + y % self.size_y

    def shift(self, step_x, step_y):
        pairs = []
        for x in range(self.size_x):
            for y in range(self.size_y):
                target = self.device[(x + step_x) % self.size_x, (y + step_y) % self.size_y]
                pairs.append((int(self.device[x, y]), int(target)))
        return pairs

    def position(self):
        here = (lax.axis_index("gx"), lax.axis_index("gy"))
        return (here, (unfolded(here[0], self.size_x), here[1]))

    def at_home(self, x, y):
        return wrapped(x, self.size_x) * self.size_y + wrapped(y, self.size_y)

    def at_work(self, x, y):
        x = traced_fold(wrapped(x, self.size_x), self.size_x)
        return x * self.size_y + wrapped(y, self.size_y)


def wrapped(value, length):
    return lax.rem(value + length, length)


def unfolded(at, length):
    if length % 2:
        return at
    return jnp.where(at % 2 == 0, at // 2, length - 1 - at // 2)


def traced_fold(position, length):
    if length % 2:
        return position
    return jnp.where(position < length // 2, 2 * position, 2 * (length - 1 - position) + 1)


def split(value):
    top = value.astype(bf16)
    return (top, (value - top.astype(f32)).astype(bf16))


def mm(left, right, contract=((1,), (0,))):
    return lax.dot_general(left, right, (contract, ((), ())), preferred_element_type=f32)


def dot3(left_top, left_rest, right):
    right_top, right_rest = split(right)
    return mm(left_top, right_top) + (mm(left_top, right_rest) + mm(left_rest, right_top))


def dot_stacked(halves, rows, right):
    right_top, right_rest = split(right)
    both = mm(halves, right_top)
    return both[:rows] + (both[rows : 2 * rows] + mm(halves[:rows], right_rest))


def exact(left, right, contract=((1,), (0,))):
    rows = left.shape[0]
    top = left.astype(bf16).astype(f32)
    rest = left - top
    middle = rest.astype(bf16).astype(f32)
    parts = jnp.concatenate([top, middle, rest - middle], axis=0).astype(bf16)
    parts = mm(parts, right, contract)
    return parts[:rows] + (parts[rows : 2 * rows] + parts[2 * rows :])


def silu(value):
    half = 0.5 * value
    return half + half * jnp.tanh(half)


def iota(shape, dim):
    return lax.broadcasted_iota(jnp.int32, shape, dim)


def edge_rows(static):
    centre = jnp.concatenate([static[2:3], static[3:4]], axis=1).astype(jnp.int32)
    other = jnp.concatenate([static[4:5], static[5:6]], axis=1).astype(jnp.int32)
    ghost = jnp.bitwise_xor(other - ATOMS, 28) + ATOMS
    return (centre, jnp.where(other >= ATOMS, ghost, other))


def onehots(static):
    centre, other = edge_rows(static)
    slots = iota((2 * ATOMS, centre.shape[1]), 0)
    return ((slots == centre).astype(f32), (slots == other).astype(f32))


def incidence(at_centre, at_other):
    return ((at_centre + at_other).astype(bf16), (at_centre - at_other).astype(bf16))


def send_columns(row):
    return (iota((ATOMS, ATOMS), 0) == row[:, :ATOMS].astype(jnp.int32)).astype(bf16)


def pick_rows(rows):
    entry = (iota(rows.shape, 1) % ATOMS) // 4
    return jnp.sum(jnp.where(entry == iota(rows.shape, 0), rows, 0.0), axis=0, keepdims=True)


def stacked_features(basis, kind_centre, kind_other):
    top = basis.astype(bf16).astype(f32)
    kinds = [kind_centre, kind_other]
    stacked = [top, basis - top, top] + kinds + kinds + [jnp.zeros_like(basis)]
    return jnp.concatenate(stacked, axis=0).astype(bf16)


def contributions(hidden, env_halves, harm, factor):
    weights = dot_stacked(env_halves, env_halves.shape[0] // 2, hidden) * (0.25 * factor)
    terms = [weights * harm[m] for m in order]
    return [split(jnp.concatenate(g, axis=0)) for g in (terms[:even_count], terms[even_count:])]


def scatter(terms, picks):
    last = ((1,), (1,))
    sides = [mm(pick, top, last) + mm(pick, rest, last) for pick, (top, rest) in zip(picks, terms)]
    return jnp.concatenate(sides, axis=1)


def store_sides(items, up_ref, mid_ref, down_ref):
    for i in range(3):
        up_ref[i] = items[4 * i : 4 * i + 4]
    for i in range(2):
        mid_ref[i] = items[12 + 4 * i : 16 + 4 * i]
    for i in range(3):
        down_ref[i] = items[20 + 4 * i : 24 + 4 * i]


def load_sides(dest, base, before_ref, after_ref, up_ref, down_ref):
    for i, k in enumerate((0, 3, 5)):
        dest[base + 4 * k : base + 4 * k + 4, :] = before_ref[i]
    for i, k in enumerate((2, 4, 7)):
        dest[base + 4 * k : base + 4 * k + 4, :] = after_ref[i]
    dest[base + 4 : base + 8, :] = up_ref[1]
    dest[base + 24 : base + 28, :] = down_ref[1]


def fetch(sources, targets, semaphores):
    copies = [
        pltpu.make_async_copy(source, target, semaphores.at[i])
        for i, (source, target) in enumerate(zip(sources, targets))
    ]
    for copy in copies:
        copy.start()
    return copies


def static_kernel(*refs):
    sources, copies_ref, targets, semaphores = (refs[:5], refs[5], refs[6:11], refs[11])
    for copy in fetch(sources, targets, semaphores):
        copy.wait()
    count_ref, positions_ref, species_ref, sends_ref, edges_ref = targets
    atoms = jnp.concatenate([positions_ref[...], species_ref[...].astype(f32)], axis=0)
    lane = iota((ATOMS, LANES), 1)
    spread = (iota((ATOMS, LANES), 0) == lane % ATOMS).astype(bf16)
    atoms = jnp.concatenate([atoms, atoms], axis=0)
    part = iota((8, LANES), 1) // ATOMS == iota((8, LANES), 0)
    atoms = jnp.sum(jnp.where(part, exact(atoms, spread), 0.0), axis=0, keepdims=True)
    sends = sends_ref[...].astype(f32)
    sends = jnp.concatenate([sends, sends], axis=0)
    lane = iota((8, LANES), 1)
    spread = (iota((8, LANES), 0) == lane % ATOMS // 4).astype(bf16)
    entry = mm(sends.astype(bf16), spread)
    entry = jnp.where(lane % 4 == iota((8, LANES), 0), entry, 0.0)
    sends = jnp.sum(entry, axis=0, keepdims=True)
    edges = edges_ref[...].astype(f32)
    count = jnp.broadcast_to(count_ref[...].astype(f32), (2, LANES))
    block = jnp.concatenate(
        [
            atoms,
            sends,
            edges[0:1, :LANES],
            edges[0:1, LANES:],
            edges[1:2, :LANES],
            edges[1:2, LANES:],
            count,
        ],
        axis=0,
    )
    copies_ref[...] = jnp.broadcast_to(block[None], copies_ref.shape)


def weights_kernel(*refs):
    sources, outs, targets, semaphores = (refs[:6], refs[6:9], refs[9:15], refs[15])
    latent_top_ref, latent_rest_ref, small_ref = outs
    latent_ref, env_ref, radial_ref, centre_ref, neighbour_ref, head_ref = targets
    for copy in fetch(sources, targets, semaphores):
        copy.wait()
    for layer in range(latent_ref.shape[0]):
        top, rest = split(latent_ref[layer].T)
        latent_top_ref[layer] = top
        latent_rest_ref[layer] = rest
        top, rest = split(env_ref[layer])
        small_ref[layer] = jnp.concatenate([top, rest], axis=0)

    def halves(value):
        top = value.astype(bf16).astype(f32)
        return (top, value - top)

    radial, centre, neighbour = (halves(r[...]) for r in (radial_ref, centre_ref, neighbour_ref))
    stacked = [radial[0], radial[0], radial[1], centre[0], neighbour[0], centre[1], neighbour[1]]
    top, rest = halves(head_ref[...])
    zeros = jnp.zeros((60, top.shape[1]), f32)
    stacked = stacked + [jnp.zeros_like(radial[0]), top, rest, zeros]
    small_ref[env_ref.shape[0]] = jnp.concatenate(stacked, axis=0).astype(bf16)


def lane_pick(rows, index):
    return jnp.take_along_axis(rows, index, axis=1, mode="promise_in_bounds")


def geometry(dx, dy, dz):
    squared = dx * dx + dy * dy + dz * dz
    scale = 1.0 / jnp.sqrt(1.0 + squared)
    x, y, z = dx * scale, dy * scale, dz * scale
    root = math.sqrt(3.0)
    harm = [
        jnp.ones_like(x),
        x,
        y,
        z,
        root * x * y,
        root * y * z,
        0.5 * (3.0 * z * z - 1.0),
        root * x * z,
        0.5 * root * (x * x - y * y),
    ]
    return ((x, y, z), jnp.sqrt(squared), harm)


def first_hidden(length, kind_centre, kind_other, embed):
    rows = iota((8, length.shape[1]), 0)
    basis = jnp.exp(-2.0 * (length - 0.5 * rows.astype(f32)) ** 2)
    kinds = [(rows == (kind + 0.5).astype(jnp.int32)).astype(f32) for kind in (kind_centre, kind_other)]
    return silu(mm(embed, stacked_features(basis, *kinds)))


def near_offsets(length, reach):
    offsets, seen = ([], set())
    for distance in range(reach + 1):
        for offset in (distance, -distance):
            if offset % length not in seen:
                seen.add(offset % length)
                offsets.append(offset)
    return offsets


def near_domains(layout, reach):
    found = [
        (x, y) for x in near_offsets(layout.size_x, reach) for y in near_offsets(layout.size_y, reach)
    ]
    return sorted(found, key=lambda at: max(abs(at[0]), abs(at[1])))


def look_up(gathered_ref, home_of, offset):
    home = home_of(*offset)
    static = gathered_ref[home]
    around = [home_of(offset[0] - offset_x[k], offset[1] - offset_y[k]) for k in range(8)]
    nearby = [gathered_ref[at] for at in around]
    lane = iota((8, LANES), 1)
    row = iota((8, LANES), 0)
    group = lane % ATOMS // 4
    sends = pick_rows(jnp.concatenate([tile[1:2] for tile in nearby], axis=0))
    sends = jnp.broadcast_to(sends, (8, LANES)).astype(jnp.int32)
    atoms = jnp.concatenate([tile[0:1] for tile in nearby], axis=0)
    ghosts = pick_rows(lane_pick(atoms, lane // ATOMS * ATOMS + sends))
    ghosts = jnp.broadcast_to(ghosts, (8, LANES))
    owner = jnp.zeros((8, LANES), jnp.int32)
    for k in range(8):
        owner = jnp.where(group == k, around[k], owner)
    entries = (owner * ATOMS + sends + 1).astype(f32)
    own = jnp.broadcast_to(static[0:1], (8, LANES))
    first = row % 4 * ATOMS
    tiles = []
    for half in range(2):
        centre = jnp.broadcast_to(static[2 + half : 3 + half], (8, LANES)).astype(jnp.int32)
        other = jnp.broadcast_to(static[4 + half : 5 + half], (8, LANES)).astype(jnp.int32)
        place = jnp.bitwise_and(other, ATOMS - 1)
        entry = jnp.bitwise_xor(place, 28)
        outside = other >= ATOMS
        start = lane_pick(own, first + centre)
        finish = jnp.where(outside, lane_pick(ghosts, first + entry), lane_pick(own, first + place))
        at_start = (home * ATOMS + 1 + centre).astype(f32)
        at_finish = jnp.where(
            outside, lane_pick(entries, entry), (home * ATOMS + 1 + place).astype(f32)
        )
        tile = jnp.where(row < 3, finish - start, finish)
        tile = jnp.where(row == 3, start, tile)
        tile = jnp.where(row == 4, at_start, tile)
        tile = jnp.where(row == 5, at_finish, tile)
        live = (lane + half * LANES < 2 * LANES // ATOMS * static[6:7].astype(jnp.int32)).astype(f32)
        tiles.append(jnp.where(row == 6, live, tile))
    return (tiles, entries, static)


def pack(rows_ref, chosen_ref, packed_ref, count):
    chosen = chosen_ref[...]
    mask = chosen.astype(bf16)
    padded = chosen.shape[0]
    before = (iota((LANES, LANES), 0) <= iota((LANES, LANES), 1)).astype(bf16)
    place = (mm(mask, before) - 1.0).astype(jnp.int32)
    totals = mm(mask, jnp.ones((LANES, LANES), bf16))
    above = (iota((padded, padded), 0) > iota((padded, padded), 1)).astype(bf16)
    starts = mm(above, totals.astype(bf16))
    packed_ref[...] = jnp.zeros_like(packed_ref)
    source = iota(chosen.shape, 1)
    distance = jnp.where(chosen > 0, source - place, 0)
    for step in range(7):
        bit = 1 << step
        coming = pltpu.roll(distance, LANES - bit, 1)
        arrives = jnp.bitwise_and(coming, bit) != 0
        source = jnp.where(arrives, pltpu.roll(source, LANES - bit, 1), source)
        stays = jnp.where(jnp.bitwise_and(distance, bit) != 0, 0, distance)
        distance = jnp.where(arrives, coming, stays)
    taken = totals.astype(jnp.int32)
    lane = iota((8, LANES), 1)
    for i in range(count):
        moved = lane_pick(rows_ref[i], jnp.broadcast_to(source[i : i + 1], (8, LANES)))
        moved = jnp.where(lane < taken[i : i + 1], moved, 0.0)
        start = jnp.max(starts[i : i + 1]).astype(jnp.int32)
        shift = jnp.bitwise_and(start, LANES - 1)
        block = lax.shift_right_logical(start, 7)
        moved = pltpu.roll(moved, shift, 1)
        packed_ref[block] += jnp.where(lane >= shift, moved, 0.0)
        packed_ref[block + 1] += jnp.where(lane < shift, moved, 0.0)
    return jnp.max(starts[padded - 1 :] + totals[padded - 1 :]).astype(jnp.int32)


def env_scalars(even, odd, harm):
    blocks = [even[64 * i : 64 * i + 64] for i in range(even_count)]
    blocks += [odd[64 * i : 64 * i + 64] for i in range(3)]
    product = {m: blocks[i] * harm[m] for i, m in enumerate(order)}
    return jnp.concatenate(
        [
            product[0],
            product[1] + product[2] + product[3],
            product[4] + product[5] + product[6] + product[7] + product[8],
        ],
        axis=0,
    )


def refined(hidden, ahead, pool, harm, sums, weight_top, weight_rest):
    top, rest = split(pool)
    first = ((0,), (0,))
    width = 64 * even_count
    even = mm(top[:, :width], sums[0], first) + mm(rest[:, :width], sums[0], first)
    odd = mm(top[:, width:], sums[1], first) + mm(rest[:, width:], sums[1], first)
    return hidden + silu(ahead + dot3(weight_top, weight_rest, env_scalars(even, odd, harm)))


def front_kernel(
    layout,
    gathered_ref,
    small_ref,
    top_ref,
    rest_ref,
    hidden_ref,
    geo_ref,
    static_ref,
    home_ref,
    env_ref,
    up_ref,
    mid_ref,
    down_ref,
    rows_ref,
    chosen_ref,
    packed_ref,
    pool_ref,
    coming_ref,
    packed_in_ref,
    slots_ref,
    pool_in_ref,
):
    (here_x, here_y), (at_x, at_y) = layout.position()
    home_ref[...] = gathered_ref[layout.at_home(here_x, here_y)]

    def home_of(x, y):
        return layout.at_home(at_x + x, at_y + y)

    tiles, entries, static = look_up(gathered_ref, home_of, (0, 0))
    static_ref[...] = static
    lane = iota((1, LANES), 1)
    first_atom = home_of(0, 0) * ATOMS + 1
    slots = jnp.where(lane < ATOMS, (first_atom + lane).astype(f32), entries[0:1])
    slots = jnp.broadcast_to(slots, (LANES, LANES)).T[: 2 * ATOMS]

    named = [jnp.where(slots[ATOMS:] == tile[5:6], tile[6:7], 0.0) for tile in tiles]
    named = jnp.max(jnp.maximum(*named), axis=1, keepdims=True) > 0
    slots = jnp.concatenate([slots[:ATOMS], jnp.where(named, slots[ATOMS:], -1.0)], axis=0)

    def touches(slots, tile):
        found = jnp.where((slots == tile[4:5]) | (slots == tile[5:6]), 1.0, 0.0)
        return jnp.max(found, axis=0, keepdims=True)

    chosen_ref[...] = jnp.zeros_like(chosen_ref)
    domains = near_domains(layout, 2)
    rows = 2 * len(domains) - 2
    rows_in = coming_ref.shape[0]
    for i, offset in enumerate(domains[1:]):
        others, _, _ = look_up(gathered_ref, home_of, offset)
        for half, tile in enumerate(others):
            at = 2 * i + half
            rows_ref[at] = tile
            if at < rows_in:
                place = tile[5:6].astype(jnp.int32) - first_atom
                coming = jnp.where((place >= 0) & (place < ATOMS), tile[6:7], 0.0)
                coming_ref[at : at + 1, :] = coming
    count_in = pack(rows_ref, coming_ref, packed_in_ref, rows_in)
    tiles_in = lax.shift_right_logical(count_in + LANES - 1, 7)

    incoming = packed_in_ref[0]
    slots = jnp.concatenate([slots, jnp.broadcast_to(incoming[4:5], (LANES, LANES)).T], axis=0)

    def choose(slots):
        for at in range(rows):
            tile = rows_ref[at]
            live = tile[6:7] - coming_ref[at : at + 1, :] if at < rows_in else tile[6:7]
            row = slice(at, at + 1)
            chosen_ref[row, :] = jnp.maximum(chosen_ref[row, :], touches(slots, tile) * live)

    choose(slots)

    def add_slots(tile, carry):
        ids = jnp.broadcast_to(packed_in_ref[tile][4:5], (LANES, LANES)).T
        slots_ref[tile] = ids
        choose(ids)
        return carry

    lax.fori_loop(1, tiles_in, add_slots, 0)
    count = pack(rows_ref, chosen_ref, packed_ref, rows)

    def found_in(slots, edges):
        slots = jnp.concatenate([slots] * (edges.shape[1] // LANES), axis=1)
        return [(slots == edges[at : at + 1]).astype(f32) for at in (4, 5)]

    embed = small_ref[small_ref.shape[0] - 1][:64].astype(f32).T.astype(bf16)

    def first_terms(edges):
        units, length, harm = geometry(edges[0:1], edges[1:2], edges[2:3])
        hidden = first_hidden(length, edges[3:4], edges[7:8], embed)
        return (units, harm, hidden, contributions(hidden, small_ref[0], harm, edges[6:7]))

    edges = jnp.concatenate(tiles + [incoming], axis=1)
    units, harm, hidden, terms = first_terms(edges)
    alive = edges[6:7]
    found = found_in(slots, edges)
    pool_ref[...] = scatter(terms, incidence(*found))
    own = 2 * LANES
    geo_ref[...] = jnp.concatenate(
        [value[:, :own] for value in harm + list(units) + [alive]] + [jnp.zeros((3, own), f32)],
        axis=0,
    )

    def start_in(tile, carry):
        pool_in_ref[tile] = scatter(terms, incidence(*found_in(slots_ref[tile], edges)))
        return carry

    lax.fori_loop(1, tiles_in, start_in, 0)

    def add_edges(edges):
        _, _, _, terms = first_terms(edges)
        pool_ref[...] += scatter(terms, incidence(*found_in(slots, edges)))

        def add_in(tile, carry):
            pool_in_ref[tile] += scatter(terms, incidence(*found_in(slots_ref[tile], edges)))
            return carry

        lax.fori_loop(1, tiles_in, add_in, 0)

    def add_tile(tile, carry):
        add_edges(packed_in_ref[tile])
        return carry

    def add_block(block, carry):
        add_edges(jnp.concatenate([packed_ref[4 * block + i] for i in range(4)], axis=1))
        return carry

    lax.fori_loop(1, tiles_in, add_tile, 0)
    lax.fori_loop(0, lax.shift_right_logical(count + 511, 9), add_block, 0)

    slot = iota(found[0].shape, 0)
    edge = iota(found[0].shape, 1)
    at_slot = slot < 2 * ATOMS
    at_centre = jnp.where(
        edge < own,
        jnp.where(at_slot, found[0], 0.0),
        (slot - 2 * ATOMS == edge - own).astype(f32),
    )
    sums = incidence(at_centre, jnp.where(at_slot, found[1], 0.0))
    size = hidden.shape[0]
    ahead = dot3(top_ref[0][:, :size], rest_ref[0][:, :size], hidden)
    weight = (top_ref[0][:, size:], rest_ref[0][:, size:])
    hidden = refined(hidden, ahead, pool_ref[...], harm, sums, *weight)
    hidden_ref[...] = hidden[:, :own]
    terms = contributions(hidden, small_ref[1], harm, alive)
    env_ref[...] = scatter(terms, incidence(*[end[:ATOMS] for end in found]))
    own_top, own_rest = split(pool_ref[:ATOMS])
    first = ((0,), (0,))
    middle = 64 * even_count

    def second_in(tile, carry):
        edges = packed_in_ref[tile]
        _, harm, hidden, _ = first_terms(edges)
        at_other = (slots[:ATOMS] == edges[5:6]).astype(f32).astype(bf16)
        other = mm(own_top, at_other, first) + mm(own_rest, at_other, first)
        centre = pool_in_ref[tile].T
        even, odd = (centre[:middle] + other[:middle], centre[middle:] - other[middle:])
        scalars = jnp.concatenate([hidden, env_scalars(even, odd, harm)], axis=0)
        hidden = hidden + silu(dot3(top_ref[0], rest_ref[0], scalars))
        terms = contributions(hidden, small_ref[1], harm, 1.0)
        env_ref[...] += scatter(terms, (at_other, -at_other))
        return carry

    lax.fori_loop(1, tiles_in, second_in, 0)
    sends = send_columns(static[1:2])
    top, rest = split(env_ref[...])
    store_sides(mm(sends, top, first) + mm(sends, rest, first), up_ref, mid_ref, down_ref)


def ahead_kernel(
    hidden_ref,
    weight_top_ref,
    weight_rest_ref,
    out_hbm_ref,
    ahead_ref,
    out_top_ref,
    out_rest_ref,
    out_ref,
    semaphores,
):
    (out_copy,) = fetch([out_hbm_ref], [out_ref], semaphores)
    size = hidden_ref.shape[0]
    weight = (weight_top_ref[1][:, :size], weight_rest_ref[1][:, :size])
    ahead_ref[...] = dot3(*weight, hidden_ref[...])
    out_copy.wait()
    out_top_ref[...], out_rest_ref[...] = split(out_ref[...])


def last_kernel(
    static_ref,
    hidden_in_ref,
    ahead_ref,
    geo_ref,
    env_ref,
    before_ref,
    after_ref,
    from_up_ref,
    from_down_ref,
    weight_top_ref,
    weight_rest_ref,
    out_top_ref,
    out_rest_ref,
    small_ref,
    totals_ref,
    pool,
):
    pool[:ATOMS, :] = env_ref[...]
    load_sides(pool, ATOMS, before_ref, after_ref, from_up_ref, from_down_ref)
    at_centre, at_other = onehots(static_ref[...])
    sums = incidence(at_centre, at_other)
    harm = [geo_ref[m : m + 1] for m in range(9)]
    hidden = hidden_in_ref[...]
    size = hidden.shape[0]
    weight = (weight_top_ref[1][:, size:], weight_rest_ref[1][:, size:])
    hidden = refined(hidden, ahead_ref[...], pool[...], harm, sums, *weight)
    latent = silu(dot3(out_top_ref[...], out_rest_ref[...], hidden))
    heads = dot_stacked(small_ref[small_ref.shape[0] - 1][64:80], 2, latent)
    alive = geo_ref[12:13]
    energy = 0.5 * heads[0:1] * alive
    push = heads[1:2] * alive
    shares = jnp.concatenate(
        [energy] + [push * geo_ref[9 + i : 10 + i] for i in range(3)] + [jnp.zeros((4, energy.shape[1]), f32)],
        axis=0,
    )
    plus, minus = sums
    last = ((1,), (1,))
    part = iota((8, LANES), 1) // ATOMS == iota((8, LANES), 0)
    rows = []
    for row in range(2):
        at = slice(row * ATOMS, (row + 1) * ATOMS)
        tiled = jnp.concatenate([plus[at], minus[at], minus[at], minus[at]], axis=0)
        spread = jnp.where(part, exact(shares, tiled, last), 0.0)
        rows.append(jnp.sum(spread, axis=0, keepdims=True))
    totals_ref[...] = jnp.broadcast_to(jnp.concatenate(rows, axis=0)[None], totals_ref.shape)


def finish_kernel(layout, gathered_ref, static_ref, energy_ref, forces_ref):
    (at_x, at_y), _ = layout.position()
    own = gathered_ref[layout.at_work(at_x, at_y)][0:1]
    rows = [
        gathered_ref[layout.at_work(at_x + offset_x[k], at_y + offset_y[k])][1:2] for k in range(8)
    ]
    ghosts = pick_rows(jnp.concatenate(rows, axis=0))
    place = iota((LANES, LANES), 1)
    sends = static_ref[1:2].astype(jnp.int32)
    target = iota((LANES, LANES), 0) == place // ATOMS * ATOMS + sends
    ghosts = jnp.concatenate([ghosts] * 8, axis=0)
    total = own + exact(ghosts, target.astype(bf16), ((1,), (1,)))[0:1]
    energy_ref[...] = total[:, :ATOMS]
    for i in range(3):
        forces_ref[i : i + 1, :] = total[:, (i + 1) * ATOMS : (i + 2) * ATOMS]


def call(kernel, outs, scratch, *operands, far=(), limit=16, work=0):
    spaces = [pltpu.HBM if i in far else pltpu.VMEM for i in range(len(operands))]
    return pl.pallas_call(
        kernel,
        out_shape=[out if hasattr(out, "dtype") else jax.ShapeDtypeStruct(out, f32) for out in outs],
        in_specs=[pl.BlockSpec(memory_space=space) for space in spaces],
        out_specs=[pl.BlockSpec(memory_space=pltpu.VMEM) for _ in outs],
        scratch_shapes=scratch,
        cost_estimate=pl.CostEstimate(flops=work << 28, bytes_accessed=1 << 20, transcendentals=0)
        if work
        else None,
        compiler_params=pltpu.CompilerParams(vmem_limit_bytes=limit * 1024 * 1024),
    )(*operands)


def fetched(operands):
    buffers = [pltpu.VMEM(value.shape, value.dtype) for value in operands]
    return buffers + [pltpu.SemaphoreType.DMA((len(operands),))]


def to_all(copies):
    return lax.all_to_all(copies, ("gx", "gy"), 0, 0, tiled=True)


def exchange(layout, sides, step):
    up, mid, down = sides
    axes = ("gx", "gy")
    up = lax.ppermute(up, axes, layout.shift(step, 0))
    down = lax.ppermute(down, axes, layout.shift(-step, 0))
    to_before = jnp.stack([up[0], mid[0], down[0]])
    to_after = jnp.stack([up[2], mid[1], down[2]])
    before = lax.ppermute(to_before, axes, layout.shift(0, step))
    after = lax.ppermute(to_after, axes, layout.shift(0, -step))
    return (before, after, up, down)


def local(
    layout,
    positions,
    species,
    atom_count,
    send_list,
    edges,
    centre_embed,
    neighbour_embed,
    radial_weight,
    env_weight,
    latent_weight,
    out_weight,
    head_weight,
):
    count_edges = edges.shape[2]
    features = out_weight.shape[0]
    rows = 9 * env_weight.shape[1]
    statics = [
        atom_count[None],
        positions,
        species[None],
        jnp.transpose(send_list[0]),
        edges[0],
    ]
    (copies,) = call(
        static_kernel,
        [(layout.count, 8, LANES)],
        fetched(statics),
        *statics,
        far=range(5),
        limit=60,
    )
    layers, channels = env_weight.shape[:2]

    def half(*shape):
        return jax.ShapeDtypeStruct(shape, bf16)

    weights = [
        jnp.transpose(latent_weight, (0, 2, 1)),
        env_weight,
        radial_weight.T,
        centre_embed.T,
        neighbour_embed.T,
        head_weight,
    ]
    latent_top, latent_rest, small = call(
        weights_kernel,
        [half(*latent_weight.shape)] * 2 + [half(layers + 1, 2 * channels, features)],
        fetched(weights),
        *weights,
        far=range(6),
        limit=44,
    )
    gathered = to_all(copies)
    sides = [(ATOMS, rows), (3, 4, rows), (2, 4, rows), (3, 4, rows)]
    geo_shape = (16, count_edges)
    hidden_shape = (features, count_edges)
    domains = len(near_domains(layout, 2))
    rows_in = 2 * len(near_domains(layout, 1)) - 2
    padded = -(-(2 * domains - 2) // 8) * 8
    scratch = [
        pltpu.VMEM((2 * domains - 2, 8, LANES), f32),
        pltpu.VMEM((padded, LANES), f32),
        pltpu.VMEM((2 * domains + 4, 8, LANES), f32),
        pltpu.VMEM((2 * ATOMS + LANES, rows), f32),
        pltpu.VMEM((rows_in, LANES), f32),
        pltpu.VMEM((rows_in + 2, 8, LANES), f32),
        pltpu.VMEM((rows_in, LANES, LANES), f32),
        pltpu.VMEM((rows_in, LANES, rows), f32),
    ]
    hidden, geo, mine, home, env, *out = call(
        functools.partial(front_kernel, layout),
        [hidden_shape, geo_shape, (8, LANES), (8, LANES)] + sides,
        scratch,
        gathered,
        small,
        latent_top,
        latent_rest,
        limit=44,
    )
    ahead, out_top, out_rest = call(
        ahead_kernel,
        [hidden_shape] + [half(*out_weight.shape)] * 2,
        fetched([out_weight]),
        hidden,
        latent_top,
        latent_rest,
        out_weight,
        far=(3,),
        work=3,
    )
    ghosts = exchange(layout, out, -1)
    pool = [pltpu.VMEM((2 * ATOMS, rows), f32)]
    (totals,) = call(
        last_kernel,
        [(layout.count, 2, LANES)],
        pool,
        mine,
        hidden,
        ahead,
        geo,
        env,
        *ghosts,
        latent_top,
        latent_rest,
        out_top,
        out_rest,
        small,
    )
    totals = to_all(totals)
    energy, forces = call(
        functools.partial(finish_kernel, layout),
        [(1, ATOMS), (3, ATOMS)],
        [],
        totals,
        home,
    )
    return (energy.reshape(-1), forces)


def solution(mesh):
    layout = Layout(mesh.shape["gx"], mesh.shape["gy"])
    placed = (
        P(None, ("gx", "gy")),
        P(("gx", "gy")),
        P(("gx", "gy")),
        P(("gx", "gy"), None, None),
        P(("gx", "gy"), None, None),
        P(),
        P(),
        P(),
        P(),
        P(),
        P(),
        P(),
    )
    return jax.shard_map(
        functools.partial(local, layout),
        mesh=mesh,
        in_specs=placed,
        out_specs=(P(("gx", "gy")), P(None, ("gx", "gy"))),
        check_vma=False,
    )
```

```python
import functools
import math

import jax
import jax.numpy as jnp
import numpy as np
from jax import lax
from jax.experimental import pallas as pl
from jax.experimental.pallas import tpu as pltpu
from jax.sharding import PartitionSpec as P

offset_x = (-1, -1, -1, 0, 0, 1, 1, 1)
offset_y = (-1, 0, 1, -1, 1, -1, 0, 1)
f32 = jnp.float32
bf16 = jnp.bfloat16
highest = lax.Precision.HIGHEST
order = (0, 4, 5, 6, 7, 8, 1, 2, 3)
even_count = 6
ATOMS = 32
LANES = 128


def folded(position, length):
    if length % 2:
        return position
    half = length // 2
    return 2 * position if position < half else 2 * (length - 1 - position) + 1


class Layout:
    def __init__(self, size_x, size_y):
        self.size_x, self.size_y = size_x, size_y
        self.count = size_x * size_y
        self.device = np.zeros((size_x, size_y), np.int32)
        self.domain = np.zeros((self.count, 2), np.int32)
        for x in range(size_x):
            for y in range(size_y):
                at = folded(x, size_x) * size_y + y
                self.device[x, y] = at
                self.domain[at] = (x, y)

    def home(self, x, y):
        return (x % self.size_x) * self.size_y + y % self.size_y

    def shift(self, step_x, step_y):
        pairs = []
        for x in range(self.size_x):
            for y in range(self.size_y):
                target = self.device[(x + step_x) % self.size_x, (y + step_y) % self.size_y]
                pairs.append((int(self.device[x, y]), int(target)))
        return pairs

    def position(self):
        here = (lax.axis_index("gx"), lax.axis_index("gy"))
        return (here, (unfolded(here[0], self.size_x), here[1]))

    def at_home(self, x, y):
        return wrapped(x, self.size_x) * self.size_y + wrapped(y, self.size_y)

    def at_work(self, x, y):
        x = traced_fold(wrapped(x, self.size_x), self.size_x)
        return x * self.size_y + wrapped(y, self.size_y)


def wrapped(value, length):
    return lax.rem(value + length, length)


def unfolded(at, length):
    if length % 2:
        return at
    return jnp.where(at % 2 == 0, at // 2, length - 1 - at // 2)


def traced_fold(position, length):
    if length % 2:
        return position
    return jnp.where(position < length // 2, 2 * position, 2 * (length - 1 - position) + 1)


def split(value):
    top = value.astype(bf16)
    return (top, (value - top.astype(f32)).astype(bf16))


def mm(left, right, contract=((1,), (0,))):
    return lax.dot_general(left, right, (contract, ((), ())), preferred_element_type=f32)


def dot3(left_top, left_rest, right):
    right_top, right_rest = split(right)
    return mm(left_top, right_top) + (mm(left_top, right_rest) + mm(left_rest, right_top))


def dot_stacked(halves, rows, right):
    right_top, right_rest = split(right)
    both = mm(halves, right_top)
    return both[:rows] + (both[rows : 2 * rows] + mm(halves[:rows], right_rest))


def exact(left, right, contract=((1,), (0,))):
    rows = left.shape[0]
    top = left.astype(bf16).astype(f32)
    rest = left - top
    middle = rest.astype(bf16).astype(f32)
    parts = jnp.concatenate([top, middle, rest - middle], axis=0).astype(bf16)
    parts = mm(parts, right, contract)
    return parts[:rows] + (parts[rows : 2 * rows] + parts[2 * rows :])


def silu(value):
    half = 0.5 * value
    return half + half * jnp.tanh(half)


def iota(shape, dim):
    return lax.broadcasted_iota(jnp.int32, shape, dim)


def edge_rows(static):
    centre = jnp.concatenate([static[2:3], static[3:4]], axis=1).astype(jnp.int32)
    other = jnp.concatenate([static[4:5], static[5:6]], axis=1).astype(jnp.int32)
    ghost = jnp.bitwise_xor(other - ATOMS, 28) + ATOMS
    return (centre, jnp.where(other >= ATOMS, ghost, other))


def onehots(static):
    centre, other = edge_rows(static)
    slots = iota((2 * ATOMS, centre.shape[1]), 0)
    return ((slots == centre).astype(f32), (slots == other).astype(f32))


def incidence(at_centre, at_other):
    return ((at_centre + at_other).astype(bf16), (at_centre - at_other).astype(bf16))


def send_columns(row):
    return (iota((ATOMS, ATOMS), 0) == row[:, :ATOMS].astype(jnp.int32)).astype(bf16)


def pick_rows(rows):
    entry = (iota(rows.shape, 1) % ATOMS) // 4
    return jnp.sum(jnp.where(entry == iota(rows.shape, 0), rows, 0.0), axis=0, keepdims=True)


def stacked_features(basis, kind_centre, kind_other):
    top = basis.astype(bf16).astype(f32)
    kinds = [kind_centre, kind_other]
    stacked = [top, basis - top, top] + kinds + kinds + [jnp.zeros_like(basis)]
    return jnp.concatenate(stacked, axis=0).astype(bf16)


def contributions(hidden, env_halves, harm, factor):
    weights = dot_stacked(env_halves, env_halves.shape[0] // 2, hidden) * (0.25 * factor)
    terms = [weights * harm[m] for m in order]
    return [split(jnp.concatenate(g, axis=0)) for g in (terms[:even_count], terms[even_count:])]


def scatter(terms, picks):
    last = ((1,), (1,))
    sides = [mm(pick, top, last) + mm(pick, rest, last) for pick, (top, rest) in zip(picks, terms)]
    return jnp.concatenate(sides, axis=1)


def store_sides(items, up_ref, mid_ref, down_ref):
    for i in range(3):
        up_ref[i] = items[4 * i : 4 * i + 4]
    for i in range(2):
        mid_ref[i] = items[12 + 4 * i : 16 + 4 * i]
    for i in range(3):
        down_ref[i] = items[20 + 4 * i : 24 + 4 * i]


def load_sides(dest, base, before_ref, after_ref, up_ref, down_ref):
    for i, k in enumerate((0, 3, 5)):
        dest[base + 4 * k : base + 4 * k + 4, :] = before_ref[i]
    for i, k in enumerate((2, 4, 7)):
        dest[base + 4 * k : base + 4 * k + 4, :] = after_ref[i]
    dest[base + 4 : base + 8, :] = up_ref[1]
    dest[base + 24 : base + 28, :] = down_ref[1]


def fetch(sources, targets, semaphores):
    copies = [
        pltpu.make_async_copy(source, target, semaphores.at[i])
        for i, (source, target) in enumerate(zip(sources, targets))
    ]
    for copy in copies:
        copy.start()
    return copies


def static_kernel(*refs):
    sources, copies_ref, targets, semaphores = (refs[:5], refs[5], refs[6:11], refs[11])
    for copy in fetch(sources, targets, semaphores):
        copy.wait()
    count_ref, positions_ref, species_ref, sends_ref, edges_ref = targets
    atoms = jnp.concatenate([positions_ref[...], species_ref[...].astype(f32)], axis=0)
    lane = iota((ATOMS, LANES), 1)
    spread = (iota((ATOMS, LANES), 0) == lane % ATOMS).astype(bf16)
    atoms = jnp.concatenate([atoms, atoms], axis=0)
    part = iota((8, LANES), 1) // ATOMS == iota((8, LANES), 0)
    atoms = jnp.sum(jnp.where(part, exact(atoms, spread), 0.0), axis=0, keepdims=True)
    sends = sends_ref[...].astype(f32)
    sends = jnp.concatenate([sends, sends], axis=0)
    lane = iota((8, LANES), 1)
    spread = (iota((8, LANES), 0) == lane % ATOMS // 4).astype(bf16)
    entry = mm(sends.astype(bf16), spread)
    entry = jnp.where(lane % 4 == iota((8, LANES), 0), entry, 0.0)
    sends = jnp.sum(entry, axis=0, keepdims=True)
    edges = edges_ref[...].astype(f32)
    count = jnp.broadcast_to(count_ref[...].astype(f32), (2, LANES))
    block = jnp.concatenate(
        [
            atoms,
            sends,
            edges[0:1, :LANES],
            edges[0:1, LANES:],
            edges[1:2, :LANES],
            edges[1:2, LANES:],
            count,
        ],
        axis=0,
    )
    copies_ref[...] = jnp.broadcast_to(block[None], copies_ref.shape)


def weights_kernel(*refs):
    sources, outs, targets, semaphores = (refs[:2], refs[2:5], refs[5:7], refs[7])
    latent_top_ref, latent_rest_ref, small_ref = outs
    latent_ref, joined_ref = targets
    layers, twice = (latent_ref.shape[0], small_ref.shape[1])
    channels = twice // 2
    for copy in fetch(sources, targets, semaphores):
        copy.wait()
    for layer in range(latent_ref.shape[0]):
        top, rest = split(latent_ref[layer].T)
        latent_top_ref[layer] = top
        latent_rest_ref[layer] = rest
        at = 24 + layer * channels
        top, rest = split(joined_ref[at : at + channels, :])
        small_ref[layer] = jnp.concatenate([top, rest], axis=0)

    def halves(value):
        top = value.astype(bf16).astype(f32)
        return (top, value - top)

    embeds = [joined_ref[8 * i : 8 * i + 8, :] for i in range(3)]
    radial, centre, neighbour = (halves(value) for value in embeds)
    stacked = [radial[0], radial[0], radial[1], centre[0], neighbour[0], centre[1], neighbour[1]]
    top, rest = halves(joined_ref[24 + layers * channels :, :])
    zeros = jnp.zeros((60, top.shape[1]), f32)
    stacked = stacked + [jnp.zeros_like(radial[0]), top, rest, zeros]
    small_ref[layers] = jnp.concatenate(stacked, axis=0).astype(bf16)


def lane_pick(rows, index):
    return jnp.take_along_axis(rows, index, axis=1, mode="promise_in_bounds")


def geometry(dx, dy, dz):
    squared = dx * dx + dy * dy + dz * dz
    scale = 1.0 / jnp.sqrt(1.0 + squared)
    x, y, z = dx * scale, dy * scale, dz * scale
    root = math.sqrt(3.0)
    harm = [
        jnp.ones_like(x),
        x,
        y,
        z,
        root * x * y,
        root * y * z,
        0.5 * (3.0 * z * z - 1.0),
        root * x * z,
        0.5 * root * (x * x - y * y),
    ]
    return ((x, y, z), jnp.sqrt(squared), harm)


def first_hidden(length, kind_centre, kind_other, embed):
    rows = iota((8, length.shape[1]), 0)
    basis = jnp.exp(-2.0 * (length - 0.5 * rows.astype(f32)) ** 2)
    kinds = [(rows == (kind + 0.5).astype(jnp.int32)).astype(f32) for kind in (kind_centre, kind_other)]
    return silu(mm(embed, stacked_features(basis, *kinds)))


def near_offsets(length, reach):
    offsets, seen = ([], set())
    for distance in range(reach + 1):
        for offset in (distance, -distance):
            if offset % length not in seen:
                seen.add(offset % length)
                offsets.append(offset)
    return offsets


def near_domains(layout, reach):
    found = [
        (x, y) for x in near_offsets(layout.size_x, reach) for y in near_offsets(layout.size_y, reach)
    ]
    return sorted(found, key=lambda at: max(abs(at[0]), abs(at[1])))


def look_up(gathered_ref, home_of, offset):
    home = home_of(*offset)
    static = gathered_ref[home]
    around = [home_of(offset[0] - offset_x[k], offset[1] - offset_y[k]) for k in range(8)]
    nearby = [gathered_ref[at] for at in around]
    lane = iota((8, LANES), 1)
    row = iota((8, LANES), 0)
    group = lane % ATOMS // 4
    sends = pick_rows(jnp.concatenate([tile[1:2] for tile in nearby], axis=0))
    sends = jnp.broadcast_to(sends, (8, LANES)).astype(jnp.int32)
    atoms = jnp.concatenate([tile[0:1] for tile in nearby], axis=0)
    ghosts = pick_rows(lane_pick(atoms, lane // ATOMS * ATOMS + sends))
    ghosts = jnp.broadcast_to(ghosts, (8, LANES))
    owner = jnp.zeros((8, LANES), jnp.int32)
    for k in range(8):
        owner = jnp.where(group == k, around[k], owner)
    entries = (owner * ATOMS + sends + 1).astype(f32)
    own = jnp.broadcast_to(static[0:1], (8, LANES))
    first = row % 4 * ATOMS
    tiles = []
    for half in range(2):
        centre = jnp.broadcast_to(static[2 + half : 3 + half], (8, LANES)).astype(jnp.int32)
        other = jnp.broadcast_to(static[4 + half : 5 + half], (8, LANES)).astype(jnp.int32)
        place = jnp.bitwise_and(other, ATOMS - 1)
        entry = jnp.bitwise_xor(place, 28)
        outside = other >= ATOMS
        start = lane_pick(own, first + centre)
        finish = jnp.where(outside, lane_pick(ghosts, first + entry), lane_pick(own, first + place))
        at_start = (home * ATOMS + 1 + centre).astype(f32)
        at_finish = jnp.where(
            outside, lane_pick(entries, entry), (home * ATOMS + 1 + place).astype(f32)
        )
        tile = jnp.where(row < 3, finish - start, finish)
        tile = jnp.where(row == 3, start, tile)
        tile = jnp.where(row == 4, at_start, tile)
        tile = jnp.where(row == 5, at_finish, tile)
        live = (lane + half * LANES < 2 * LANES // ATOMS * static[6:7].astype(jnp.int32)).astype(f32)
        tiles.append(jnp.where(row == 6, live, tile))
    return (tiles, entries, static)


def pack(rows_ref, chosen_ref, packed_ref, count):
    chosen = chosen_ref[...]
    mask = chosen.astype(bf16)
    padded = chosen.shape[0]
    before = (iota((LANES, LANES), 0) <= iota((LANES, LANES), 1)).astype(bf16)
    place = (mm(mask, before) - 1.0).astype(jnp.int32)
    totals = mm(mask, jnp.ones((LANES, LANES), bf16))
    above = (iota((padded, padded), 0) > iota((padded, padded), 1)).astype(bf16)
    starts = mm(above, totals.astype(bf16))
    packed_ref[...] = jnp.zeros_like(packed_ref)
    source = iota(chosen.shape, 1)
    distance = jnp.where(chosen > 0, source - place, 0)
    for step in range(7):
        bit = 1 << step
        coming = pltpu.roll(distance, LANES - bit, 1)
        arrives = jnp.bitwise_and(coming, bit) != 0
        source = jnp.where(arrives, pltpu.roll(source, LANES - bit, 1), source)
        stays = jnp.where(jnp.bitwise_and(distance, bit) != 0, 0, distance)
        distance = jnp.where(arrives, coming, stays)
    taken = totals.astype(jnp.int32)
    lane = iota((8, LANES), 1)
    for i in range(count):
        moved = lane_pick(rows_ref[i], jnp.broadcast_to(source[i : i + 1], (8, LANES)))
        moved = jnp.where(lane < taken[i : i + 1], moved, 0.0)
        start = jnp.max(starts[i : i + 1]).astype(jnp.int32)
        shift = jnp.bitwise_and(start, LANES - 1)
        block = lax.shift_right_logical(start, 7)
        moved = pltpu.roll(moved, shift, 1)
        packed_ref[block] += jnp.where(lane >= shift, moved, 0.0)
        packed_ref[block + 1] += jnp.where(lane < shift, moved, 0.0)
    return jnp.max(starts[padded - 1 :] + totals[padded - 1 :]).astype(jnp.int32)


def env_scalars(even, odd, harm):
    blocks = [even[64 * i : 64 * i + 64] for i in range(even_count)]
    blocks += [odd[64 * i : 64 * i + 64] for i in range(3)]
    product = {m: blocks[i] * harm[m] for i, m in enumerate(order)}
    return jnp.concatenate(
        [
            product[0],
            product[1] + product[2] + product[3],
            product[4] + product[5] + product[6] + product[7] + product[8],
        ],
        axis=0,
    )


def refined(hidden, ahead, pool, harm, sums, weight_top, weight_rest):
    top, rest = split(pool)
    first = ((0,), (0,))
    width = 64 * even_count
    even = mm(top[:, :width], sums[0], first) + mm(rest[:, :width], sums[0], first)
    odd = mm(top[:, width:], sums[1], first) + mm(rest[:, width:], sums[1], first)
    return hidden + silu(ahead + dot3(weight_top, weight_rest, env_scalars(even, odd, harm)))


def front_kernel(
    layout,
    gathered_ref,
    small_ref,
    top_ref,
    rest_ref,
    hidden_ref,
    geo_ref,
    static_ref,
    home_ref,
    env_ref,
    up_ref,
    mid_ref,
    down_ref,
    rows_ref,
    chosen_ref,
    packed_ref,
    pool_ref,
    coming_ref,
    packed_in_ref,
    slots_ref,
    pool_in_ref,
):
    (here_x, here_y), (at_x, at_y) = layout.position()
    home_ref[...] = gathered_ref[layout.at_home(here_x, here_y)]

    def home_of(x, y):
        return layout.at_home(at_x + x, at_y + y)

    tiles, entries, static = look_up(gathered_ref, home_of, (0, 0))
    static_ref[...] = static
    lane = iota((1, LANES), 1)
    first_atom = home_of(0, 0) * ATOMS + 1
    slots = jnp.where(lane < ATOMS, (first_atom + lane).astype(f32), entries[0:1])
    slots = jnp.broadcast_to(slots, (LANES, LANES)).T[: 2 * ATOMS]

    named = [jnp.where(slots[ATOMS:] == tile[5:6], tile[6:7], 0.0) for tile in tiles]
    named = jnp.max(jnp.maximum(*named), axis=1, keepdims=True) > 0
    slots = jnp.concatenate([slots[:ATOMS], jnp.where(named, slots[ATOMS:], -1.0)], axis=0)

    def touches(slots, tile, nearest):
        found = slots == tile[5:6]
        if nearest:
            found = found | (slots == tile[4:5])
        return jnp.max(jnp.where(found, 1.0, 0.0), axis=0, keepdims=True)

    chosen_ref[...] = jnp.zeros_like(chosen_ref)
    domains = near_domains(layout, 2)
    rows = 2 * len(domains) - 2
    rows_in = coming_ref.shape[0]
    for i, offset in enumerate(domains[1:]):
        others, _, _ = look_up(gathered_ref, home_of, offset)
        for half, tile in enumerate(others):
            at = 2 * i + half
            rows_ref[at] = tile
            if at < rows_in:
                place = tile[5:6].astype(jnp.int32) - first_atom
                coming = jnp.where((place >= 0) & (place < ATOMS), tile[6:7], 0.0)
                coming_ref[at : at + 1, :] = coming
    count_in = pack(rows_ref, coming_ref, packed_in_ref, rows_in)
    tiles_in = lax.shift_right_logical(count_in + LANES - 1, 7)

    incoming = packed_in_ref[0]
    slots = jnp.concatenate([slots, jnp.broadcast_to(incoming[4:5], (LANES, LANES)).T], axis=0)

    def choose(slots):
        for at in range(rows):
            tile = rows_ref[at]
            live = tile[6:7] - coming_ref[at : at + 1, :] if at < rows_in else tile[6:7]
            row = slice(at, at + 1)
            found = touches(slots, tile, at < rows_in) * live
            chosen_ref[row, :] = jnp.maximum(chosen_ref[row, :], found)

    choose(slots)

    def add_slots(tile, carry):
        ids = jnp.broadcast_to(packed_in_ref[tile][4:5], (LANES, LANES)).T
        slots_ref[tile] = ids
        choose(ids)
        return carry

    lax.fori_loop(1, tiles_in, add_slots, 0)
    count = pack(rows_ref, chosen_ref, packed_ref, rows)

    def found_in(slots, edges):
        slots = jnp.concatenate([slots] * (edges.shape[1] // LANES), axis=1)
        return [(slots == edges[at : at + 1]).astype(f32) for at in (4, 5)]

    embed = small_ref[small_ref.shape[0] - 1][:64].astype(f32).T.astype(bf16)

    def first_terms(edges):
        units, length, harm = geometry(edges[0:1], edges[1:2], edges[2:3])
        hidden = first_hidden(length, edges[3:4], edges[7:8], embed)
        return (units, harm, hidden, contributions(hidden, small_ref[0], harm, edges[6:7]))

    edges = jnp.concatenate(tiles + [incoming], axis=1)
    units, harm, hidden, terms = first_terms(edges)
    alive = edges[6:7]
    found = found_in(slots, edges)
    pool_ref[...] = scatter(terms, incidence(*found))
    own = 2 * LANES
    geo_ref[...] = jnp.concatenate(
        [value[:, :own] for value in harm + list(units) + [alive]] + [jnp.zeros((3, own), f32)],
        axis=0,
    )

    def start_in(tile, carry):
        pool_in_ref[tile] = scatter(terms, incidence(*found_in(slots_ref[tile], edges)))
        return carry

    lax.fori_loop(1, tiles_in, start_in, 0)

    def add_edges(edges):
        _, _, _, terms = first_terms(edges)
        pool_ref[...] += scatter(terms, incidence(*found_in(slots, edges)))

        def add_in(tile, carry):
            pool_in_ref[tile] += scatter(terms, incidence(*found_in(slots_ref[tile], edges)))
            return carry

        lax.fori_loop(1, tiles_in, add_in, 0)

    def add_tile(tile, carry):
        add_edges(packed_in_ref[tile])
        return carry

    def add_block(block, carry):
        add_edges(jnp.concatenate([packed_ref[4 * block + i] for i in range(4)], axis=1))
        return carry

    lax.fori_loop(1, tiles_in, add_tile, 0)
    lax.fori_loop(0, lax.shift_right_logical(count + 511, 9), add_block, 0)

    slot = iota(found[0].shape, 0)
    edge = iota(found[0].shape, 1)
    at_slot = slot < 2 * ATOMS
    at_centre = jnp.where(
        edge < own,
        jnp.where(at_slot, found[0], 0.0),
        (slot - 2 * ATOMS == edge - own).astype(f32),
    )
    sums = incidence(at_centre, jnp.where(at_slot, found[1], 0.0))
    size = hidden.shape[0]
    ahead = dot3(top_ref[0][:, :size], rest_ref[0][:, :size], hidden)
    weight = (top_ref[0][:, size:], rest_ref[0][:, size:])
    hidden = refined(hidden, ahead, pool_ref[...], harm, sums, *weight)
    hidden_ref[...] = hidden[:, :own]
    terms = contributions(hidden, small_ref[1], harm, alive)
    env_ref[...] = scatter(terms, incidence(*[end[:ATOMS] for end in found]))
    own_top, own_rest = split(pool_ref[:ATOMS])
    first = ((0,), (0,))
    middle = 64 * even_count

    def second_in(tile, carry):
        edges = packed_in_ref[tile]
        _, harm, hidden, _ = first_terms(edges)
        at_other = (slots[:ATOMS] == edges[5:6]).astype(f32).astype(bf16)
        other = mm(own_top, at_other, first) + mm(own_rest, at_other, first)
        centre = pool_in_ref[tile].T
        even, odd = (centre[:middle] + other[:middle], centre[middle:] - other[middle:])
        scalars = jnp.concatenate([hidden, env_scalars(even, odd, harm)], axis=0)
        hidden = hidden + silu(dot3(top_ref[0], rest_ref[0], scalars))
        terms = contributions(hidden, small_ref[1], harm, 1.0)
        env_ref[...] += scatter(terms, (at_other, -at_other))
        return carry

    lax.fori_loop(1, tiles_in, second_in, 0)
    sends = send_columns(static[1:2])
    top, rest = split(env_ref[...])
    store_sides(mm(sends, top, first) + mm(sends, rest, first), up_ref, mid_ref, down_ref)


def ahead_kernel(
    hidden_ref,
    weight_top_ref,
    weight_rest_ref,
    out_hbm_ref,
    ahead_ref,
    out_top_ref,
    out_rest_ref,
    out_ref,
    semaphores,
):
    (out_copy,) = fetch([out_hbm_ref], [out_ref], semaphores)
    size = hidden_ref.shape[0]
    weight = (weight_top_ref[1][:, :size], weight_rest_ref[1][:, :size])
    ahead_ref[...] = dot3(*weight, hidden_ref[...])
    out_copy.wait()
    out_top_ref[...], out_rest_ref[...] = split(out_ref[...])


def last_kernel(
    static_ref,
    hidden_in_ref,
    ahead_ref,
    geo_ref,
    env_ref,
    before_ref,
    after_ref,
    from_up_ref,
    from_down_ref,
    weight_top_ref,
    weight_rest_ref,
    out_top_ref,
    out_rest_ref,
    small_ref,
    totals_ref,
    pool,
):
    pool[:ATOMS, :] = env_ref[...]
    load_sides(pool, ATOMS, before_ref, after_ref, from_up_ref, from_down_ref)
    at_centre, at_other = onehots(static_ref[...])
    sums = incidence(at_centre, at_other)
    harm = [geo_ref[m : m + 1] for m in range(9)]
    hidden = hidden_in_ref[...]
    size = hidden.shape[0]
    weight = (weight_top_ref[1][:, size:], weight_rest_ref[1][:, size:])
    hidden = refined(hidden, ahead_ref[...], pool[...], harm, sums, *weight)
    latent = silu(dot3(out_top_ref[...], out_rest_ref[...], hidden))
    heads = dot_stacked(small_ref[small_ref.shape[0] - 1][64:80], 2, latent)
    alive = geo_ref[12:13]
    energy = 0.5 * heads[0:1] * alive
    push = heads[1:2] * alive
    shares = jnp.concatenate(
        [energy] + [push * geo_ref[9 + i : 10 + i] for i in range(3)] + [jnp.zeros((4, energy.shape[1]), f32)],
        axis=0,
    )
    plus, minus = sums
    last = ((1,), (1,))
    part = iota((8, LANES), 1) // ATOMS == iota((8, LANES), 0)
    rows = []
    for row in range(2):
        at = slice(row * ATOMS, (row + 1) * ATOMS)
        tiled = jnp.concatenate([plus[at], minus[at], minus[at], minus[at]], axis=0)
        spread = jnp.where(part, exact(shares, tiled, last), 0.0)
        rows.append(jnp.sum(spread, axis=0, keepdims=True))
    totals_ref[...] = jnp.broadcast_to(jnp.concatenate(rows, axis=0)[None], totals_ref.shape)


def finish_kernel(layout, gathered_ref, static_ref, energy_ref, forces_ref):
    (at_x, at_y), _ = layout.position()
    own = gathered_ref[layout.at_work(at_x, at_y)][0:1]
    rows = [
        gathered_ref[layout.at_work(at_x + offset_x[k], at_y + offset_y[k])][1:2] for k in range(8)
    ]
    ghosts = pick_rows(jnp.concatenate(rows, axis=0))
    place = iota((LANES, LANES), 1)
    sends = static_ref[1:2].astype(jnp.int32)
    target = iota((LANES, LANES), 0) == place // ATOMS * ATOMS + sends
    ghosts = jnp.concatenate([ghosts] * 8, axis=0)
    total = own + exact(ghosts, target.astype(bf16), ((1,), (1,)))[0:1]
    energy_ref[...] = total[:, :ATOMS]
    for i in range(3):
        forces_ref[i : i + 1, :] = total[:, (i + 1) * ATOMS : (i + 2) * ATOMS]


def call(kernel, outs, scratch, *operands, far=(), limit=16, work=0):
    spaces = [pltpu.HBM if i in far else pltpu.VMEM for i in range(len(operands))]
    return pl.pallas_call(
        kernel,
        out_shape=[out if hasattr(out, "dtype") else jax.ShapeDtypeStruct(out, f32) for out in outs],
        in_specs=[pl.BlockSpec(memory_space=space) for space in spaces],
        out_specs=[pl.BlockSpec(memory_space=pltpu.VMEM) for _ in outs],
        scratch_shapes=scratch,
        cost_estimate=pl.CostEstimate(flops=work << 28, bytes_accessed=1 << 20, transcendentals=0)
        if work
        else None,
        compiler_params=pltpu.CompilerParams(vmem_limit_bytes=limit * 1024 * 1024),
    )(*operands)


def fetched(operands):
    buffers = [pltpu.VMEM(value.shape, value.dtype) for value in operands]
    return buffers + [pltpu.SemaphoreType.DMA((len(operands),))]


def to_all(copies):
    return lax.all_to_all(copies, ("gx", "gy"), 0, 0, tiled=True)


def exchange(layout, sides, step):
    up, mid, down = sides
    axes = ("gx", "gy")
    up = lax.ppermute(up, axes, layout.shift(step, 0))
    down = lax.ppermute(down, axes, layout.shift(-step, 0))
    to_before = jnp.stack([up[0], mid[0], down[0]])
    to_after = jnp.stack([up[2], mid[1], down[2]])
    before = lax.ppermute(to_before, axes, layout.shift(0, step))
    after = lax.ppermute(to_after, axes, layout.shift(0, -step))
    return (before, after, up, down)


def local(
    layout,
    positions,
    species,
    atom_count,
    send_list,
    edges,
    centre_embed,
    neighbour_embed,
    radial_weight,
    env_weight,
    latent_weight,
    out_weight,
    head_weight,
):
    count_edges = edges.shape[2]
    features = out_weight.shape[0]
    rows = 9 * env_weight.shape[1]
    statics = [
        atom_count[None],
        positions,
        species[None],
        jnp.transpose(send_list[0]),
        edges[0],
    ]
    (copies,) = call(
        static_kernel,
        [(layout.count, 8, LANES)],
        fetched(statics),
        *statics,
        far=range(5),
        limit=60,
    )
    layers, channels = env_weight.shape[:2]

    def half(*shape):
        return jax.ShapeDtypeStruct(shape, bf16)

    joined = [radial_weight.T, centre_embed.T, neighbour_embed.T]
    joined += [env_weight.reshape(layers * channels, features), head_weight]
    weights = [jnp.transpose(latent_weight, (0, 2, 1)), jnp.concatenate(joined, axis=0)]
    latent_top, latent_rest, small = call(
        weights_kernel,
        [half(*latent_weight.shape)] * 2 + [half(layers + 1, 2 * channels, features)],
        fetched(weights),
        *weights,
        far=range(2),
        limit=44,
    )
    gathered = to_all(copies)
    sides = [(ATOMS, rows), (3, 4, rows), (2, 4, rows), (3, 4, rows)]
    geo_shape = (16, count_edges)
    hidden_shape = (features, count_edges)
    domains = len(near_domains(layout, 2))
    rows_in = 2 * len(near_domains(layout, 1)) - 2
    padded = -(-(2 * domains - 2) // 8) * 8
    scratch = [
        pltpu.VMEM((2 * domains - 2, 8, LANES), f32),
        pltpu.VMEM((padded, LANES), f32),
        pltpu.VMEM((2 * domains + 4, 8, LANES), f32),
        pltpu.VMEM((2 * ATOMS + LANES, rows), f32),
        pltpu.VMEM((rows_in, LANES), f32),
        pltpu.VMEM((rows_in + 2, 8, LANES), f32),
        pltpu.VMEM((rows_in, LANES, LANES), f32),
        pltpu.VMEM((rows_in, LANES, rows), f32),
    ]
    hidden, geo, mine, home, env, *out = call(
        functools.partial(front_kernel, layout),
        [hidden_shape, geo_shape, (8, LANES), (8, LANES)] + sides,
        scratch,
        gathered,
        small,
        latent_top,
        latent_rest,
        limit=44,
    )
    ahead, out_top, out_rest = call(
        ahead_kernel,
        [hidden_shape] + [half(*out_weight.shape)] * 2,
        fetched([out_weight]),
        hidden,
        latent_top,
        latent_rest,
        out_weight,
        far=(3,),
        work=3,
    )
    ghosts = exchange(layout, out, -1)
    pool = [pltpu.VMEM((2 * ATOMS, rows), f32)]
    (totals,) = call(
        last_kernel,
        [(layout.count, 2, LANES)],
        pool,
        mine,
        hidden,
        ahead,
        geo,
        env,
        *ghosts,
        latent_top,
        latent_rest,
        out_top,
        out_rest,
        small,
    )
    totals = to_all(totals)
    energy, forces = call(
        functools.partial(finish_kernel, layout),
        [(1, ATOMS), (3, ATOMS)],
        [],
        totals,
        home,
    )
    return (energy.reshape(-1), forces)


def solution(mesh):
    layout = Layout(mesh.shape["gx"], mesh.shape["gy"])
    placed = (
        P(None, ("gx", "gy")),
        P(("gx", "gy")),
        P(("gx", "gy")),
        P(("gx", "gy"), None, None),
        P(("gx", "gy"), None, None),
        P(),
        P(),
        P(),
        P(),
        P(),
        P(),
        P(),
    )
    return jax.shard_map(
        functools.partial(local, layout),
        mesh=mesh,
        in_specs=placed,
        out_specs=(P(("gx", "gy")), P(None, ("gx", "gy"))),
        check_vma=False,
    )
```

```python
import functools
import math

import jax
import jax.numpy as jnp
import numpy as np
from jax import lax
from jax.experimental import pallas as pl
from jax.experimental.pallas import tpu as pltpu
from jax.sharding import PartitionSpec as P

offset_x = (-1, -1, -1, 0, 0, 1, 1, 1)
offset_y = (-1, 0, 1, -1, 1, -1, 0, 1)
f32 = jnp.float32
bf16 = jnp.bfloat16
highest = lax.Precision.HIGHEST
order = (0, 4, 5, 6, 7, 8, 1, 2, 3)
even_count = 6
ATOMS = 32
LANES = 128


def folded(position, length):
    if length % 2:
        return position
    half = length // 2
    return 2 * position if position < half else 2 * (length - 1 - position) + 1


class Layout:
    def __init__(self, size_x, size_y):
        self.size_x, self.size_y = size_x, size_y
        self.count = size_x * size_y
        self.device = np.zeros((size_x, size_y), np.int32)
        self.domain = np.zeros((self.count, 2), np.int32)
        for x in range(size_x):
            for y in range(size_y):
                at = folded(x, size_x) * size_y + y
                self.device[x, y] = at
                self.domain[at] = (x, y)

    def home(self, x, y):
        return (x % self.size_x) * self.size_y + y % self.size_y

    def shift(self, step_x, step_y):
        pairs = []
        for x in range(self.size_x):
            for y in range(self.size_y):
                target = self.device[(x + step_x) % self.size_x, (y + step_y) % self.size_y]
                pairs.append((int(self.device[x, y]), int(target)))
        return pairs

    def position(self):
        here = (lax.axis_index("gx"), lax.axis_index("gy"))
        return (here, (unfolded(here[0], self.size_x), here[1]))

    def at_home(self, x, y):
        return wrapped(x, self.size_x) * self.size_y + wrapped(y, self.size_y)

    def at_work(self, x, y):
        x = traced_fold(wrapped(x, self.size_x), self.size_x)
        return x * self.size_y + wrapped(y, self.size_y)


def wrapped(value, length):
    return lax.rem(value + length, length)


def unfolded(at, length):
    if length % 2:
        return at
    return jnp.where(at % 2 == 0, at // 2, length - 1 - at // 2)


def traced_fold(position, length):
    if length % 2:
        return position
    return jnp.where(position < length // 2, 2 * position, 2 * (length - 1 - position) + 1)


def split(value):
    top = value.astype(bf16)
    return (top, (value - top.astype(f32)).astype(bf16))


def mm(left, right, contract=((1,), (0,))):
    return lax.dot_general(left, right, (contract, ((), ())), preferred_element_type=f32)


def dot3(left_top, left_rest, right):
    right_top, right_rest = split(right)
    return mm(left_top, right_top) + (mm(left_top, right_rest) + mm(left_rest, right_top))


def dot_stacked(halves, rows, right):
    right_top, right_rest = split(right)
    both = mm(halves, right_top)
    return both[:rows] + (both[rows : 2 * rows] + mm(halves[:rows], right_rest))


def exact(left, right, contract=((1,), (0,))):
    rows = left.shape[0]
    top = left.astype(bf16).astype(f32)
    rest = left - top
    middle = rest.astype(bf16).astype(f32)
    parts = jnp.concatenate([top, middle, rest - middle], axis=0).astype(bf16)
    parts = mm(parts, right, contract)
    return parts[:rows] + (parts[rows : 2 * rows] + parts[2 * rows :])


def silu(value):
    half = 0.5 * value
    return half + half * jnp.tanh(half)


def iota(shape, dim):
    return lax.broadcasted_iota(jnp.int32, shape, dim)


def edge_rows(static):
    centre = jnp.concatenate([static[2:3], static[3:4]], axis=1).astype(jnp.int32)
    other = jnp.concatenate([static[4:5], static[5:6]], axis=1).astype(jnp.int32)
    ghost = jnp.bitwise_xor(other - ATOMS, 28) + ATOMS
    return (centre, jnp.where(other >= ATOMS, ghost, other))


def onehots(static):
    centre, other = edge_rows(static)
    slots = iota((2 * ATOMS, centre.shape[1]), 0)
    return ((slots == centre).astype(f32), (slots == other).astype(f32))


def incidence(at_centre, at_other):
    return ((at_centre + at_other).astype(bf16), (at_centre - at_other).astype(bf16))


def send_columns(row):
    return (iota((ATOMS, ATOMS), 0) == row[:, :ATOMS].astype(jnp.int32)).astype(bf16)


def pick_rows(rows):
    entry = (iota(rows.shape, 1) % ATOMS) // 4
    return jnp.sum(jnp.where(entry == iota(rows.shape, 0), rows, 0.0), axis=0, keepdims=True)


def stacked_features(basis, kind_centre, kind_other):
    top = basis.astype(bf16).astype(f32)
    kinds = [kind_centre, kind_other]
    stacked = [top, basis - top, top] + kinds + kinds + [jnp.zeros_like(basis)]
    return jnp.concatenate(stacked, axis=0).astype(bf16)


def contributions(hidden, env_halves, harm, factor):
    weights = dot_stacked(env_halves, env_halves.shape[0] // 2, hidden) * (0.25 * factor)
    terms = [weights * harm[m] for m in order]
    return [split(jnp.concatenate(g, axis=0)) for g in (terms[:even_count], terms[even_count:])]


def scatter(terms, picks):
    last = ((1,), (1,))
    sides = [mm(pick, top, last) + mm(pick, rest, last) for pick, (top, rest) in zip(picks, terms)]
    return jnp.concatenate(sides, axis=1)


def store_sides(items, up_ref, mid_ref, down_ref):
    for i in range(3):
        up_ref[i] = items[4 * i : 4 * i + 4]
    for i in range(2):
        mid_ref[i] = items[12 + 4 * i : 16 + 4 * i]
    for i in range(3):
        down_ref[i] = items[20 + 4 * i : 24 + 4 * i]


def load_sides(dest, base, before_ref, after_ref, up_ref, down_ref):
    for i, k in enumerate((0, 3, 5)):
        dest[base + 4 * k : base + 4 * k + 4, :] = before_ref[i]
    for i, k in enumerate((2, 4, 7)):
        dest[base + 4 * k : base + 4 * k + 4, :] = after_ref[i]
    dest[base + 4 : base + 8, :] = up_ref[1]
    dest[base + 24 : base + 28, :] = down_ref[1]


def fetch(sources, targets, semaphores):
    copies = [
        pltpu.make_async_copy(source, target, semaphores.at[i])
        for i, (source, target) in enumerate(zip(sources, targets))
    ]
    for copy in copies:
        copy.start()
    return copies


def static_kernel(*refs):
    sources, copies_ref, targets, semaphores = (refs[:5], refs[5], refs[6:11], refs[11])
    for copy in fetch(sources, targets, semaphores):
        copy.wait()
    count_ref, positions_ref, species_ref, sends_ref, edges_ref = targets
    atoms = jnp.concatenate([positions_ref[...], species_ref[...].astype(f32)], axis=0)
    lane = iota((ATOMS, LANES), 1)
    spread = (iota((ATOMS, LANES), 0) == lane % ATOMS).astype(bf16)
    atoms = jnp.concatenate([atoms, atoms], axis=0)
    part = iota((8, LANES), 1) // ATOMS == iota((8, LANES), 0)
    atoms = jnp.sum(jnp.where(part, exact(atoms, spread), 0.0), axis=0, keepdims=True)
    sends = sends_ref[...].astype(f32)
    sends = jnp.concatenate([sends, sends], axis=0)
    lane = iota((8, LANES), 1)
    spread = (iota((8, LANES), 0) == lane % ATOMS // 4).astype(bf16)
    entry = mm(sends.astype(bf16), spread)
    entry = jnp.where(lane % 4 == iota((8, LANES), 0), entry, 0.0)
    sends = jnp.sum(entry, axis=0, keepdims=True)
    edges = edges_ref[...].astype(f32)
    count = jnp.broadcast_to(count_ref[...].astype(f32), (2, LANES))
    block = jnp.concatenate(
        [
            atoms,
            sends,
            edges[0:1, :LANES],
            edges[0:1, LANES:],
            edges[1:2, :LANES],
            edges[1:2, LANES:],
            count,
        ],
        axis=0,
    )
    copies_ref[...] = jnp.broadcast_to(block[None], copies_ref.shape)


def weights_kernel(*refs):
    sources, outs, targets, semaphores = (refs[:2], refs[2:4], refs[4:6], refs[6])
    latent_halves_ref, small_ref = outs
    latent_ref, joined_ref = targets
    layers, channels = (small_ref.shape[0] - 1, small_ref.shape[1] // 2)
    for copy in fetch(sources, targets, semaphores):
        copy.wait()
    latent_halves_ref[0], latent_halves_ref[1] = split(latent_ref[...].T)
    for layer in range(layers):
        at = 24 + layer * channels
        top, rest = split(joined_ref[at : at + channels, :])
        small_ref[layer] = jnp.concatenate([top, rest], axis=0)

    def halves(value):
        top = value.astype(bf16).astype(f32)
        return (top, value - top)

    embeds = [joined_ref[8 * i : 8 * i + 8, :] for i in range(3)]
    radial, centre, neighbour = (halves(value) for value in embeds)
    stacked = [radial[0], radial[0], radial[1], centre[0], neighbour[0], centre[1], neighbour[1]]
    top, rest = halves(joined_ref[24 + layers * channels :, :])
    zeros = jnp.zeros((60, top.shape[1]), f32)
    stacked = stacked + [jnp.zeros_like(radial[0]), top, rest, zeros]
    small_ref[layers] = jnp.concatenate(stacked, axis=0).astype(bf16)


def lane_pick(rows, index):
    return jnp.take_along_axis(rows, index, axis=1, mode="promise_in_bounds")


def geometry(dx, dy, dz):
    squared = dx * dx + dy * dy + dz * dz
    scale = 1.0 / jnp.sqrt(1.0 + squared)
    x, y, z = dx * scale, dy * scale, dz * scale
    root = math.sqrt(3.0)
    harm = [
        jnp.ones_like(x),
        x,
        y,
        z,
        root * x * y,
        root * y * z,
        0.5 * (3.0 * z * z - 1.0),
        root * x * z,
        0.5 * root * (x * x - y * y),
    ]
    return ((x, y, z), jnp.sqrt(squared), harm)


def first_hidden(length, kind_centre, kind_other, embed):
    rows = iota((8, length.shape[1]), 0)
    basis = jnp.exp(-2.0 * (length - 0.5 * rows.astype(f32)) ** 2)
    kinds = [(rows == (kind + 0.5).astype(jnp.int32)).astype(f32) for kind in (kind_centre, kind_other)]
    return silu(mm(embed, stacked_features(basis, *kinds)))


def near_offsets(length, reach):
    offsets, seen = ([], set())
    for distance in range(reach + 1):
        for offset in (distance, -distance):
            if offset % length not in seen:
                seen.add(offset % length)
                offsets.append(offset)
    return offsets


def near_domains(layout, reach):
    found = [
        (x, y) for x in near_offsets(layout.size_x, reach) for y in near_offsets(layout.size_y, reach)
    ]
    return sorted(found, key=lambda at: max(abs(at[0]), abs(at[1])))


def look_up(gathered_ref, home_of, offset):
    home = home_of(*offset)
    static = gathered_ref[home]
    around = [home_of(offset[0] - offset_x[k], offset[1] - offset_y[k]) for k in range(8)]
    nearby = [gathered_ref[at] for at in around]
    lane = iota((8, LANES), 1)
    row = iota((8, LANES), 0)
    group = lane % ATOMS // 4
    sends = pick_rows(jnp.concatenate([tile[1:2] for tile in nearby], axis=0))
    sends = jnp.broadcast_to(sends, (8, LANES)).astype(jnp.int32)
    atoms = jnp.concatenate([tile[0:1] for tile in nearby], axis=0)
    ghosts = pick_rows(lane_pick(atoms, lane // ATOMS * ATOMS + sends))
    ghosts = jnp.broadcast_to(ghosts, (8, LANES))
    owner = jnp.zeros((8, LANES), jnp.int32)
    for k in range(8):
        owner = jnp.where(group == k, around[k], owner)
    entries = (owner * ATOMS + sends + 1).astype(f32)
    own = jnp.broadcast_to(static[0:1], (8, LANES))
    first = row % 4 * ATOMS
    tiles = []
    for half in range(2):
        centre = jnp.broadcast_to(static[2 + half : 3 + half], (8, LANES)).astype(jnp.int32)
        other = jnp.broadcast_to(static[4 + half : 5 + half], (8, LANES)).astype(jnp.int32)
        place = jnp.bitwise_and(other, ATOMS - 1)
        entry = jnp.bitwise_xor(place, 28)
        outside = other >= ATOMS
        start = lane_pick(own, first + centre)
        finish = jnp.where(outside, lane_pick(ghosts, first + entry), lane_pick(own, first + place))
        at_start = (home * ATOMS + 1 + centre).astype(f32)
        at_finish = jnp.where(
            outside, lane_pick(entries, entry), (home * ATOMS + 1 + place).astype(f32)
        )
        tile = jnp.where(row < 3, finish - start, finish)
        tile = jnp.where(row == 3, start, tile)
        tile = jnp.where(row == 4, at_start, tile)
        tile = jnp.where(row == 5, at_finish, tile)
        live = (lane + half * LANES < 2 * LANES // ATOMS * static[6:7].astype(jnp.int32)).astype(f32)
        tiles.append(jnp.where(row == 6, live, tile))
    return (tiles, entries, static)


def pack(rows_ref, chosen_ref, packed_ref, count):
    chosen = chosen_ref[...]
    mask = chosen.astype(bf16)
    padded = chosen.shape[0]
    before = (iota((LANES, LANES), 0) <= iota((LANES, LANES), 1)).astype(bf16)
    place = (mm(mask, before) - 1.0).astype(jnp.int32)
    totals = mm(mask, jnp.ones((LANES, LANES), bf16))
    above = (iota((padded, padded), 0) > iota((padded, padded), 1)).astype(bf16)
    starts = mm(above, totals.astype(bf16))
    packed_ref[...] = jnp.zeros_like(packed_ref)
    source = iota(chosen.shape, 1)
    distance = jnp.where(chosen > 0, source - place, 0)
    for step in range(7):
        bit = 1 << step
        coming = pltpu.roll(distance, LANES - bit, 1)
        arrives = jnp.bitwise_and(coming, bit) != 0
        source = jnp.where(arrives, pltpu.roll(source, LANES - bit, 1), source)
        stays = jnp.where(jnp.bitwise_and(distance, bit) != 0, 0, distance)
        distance = jnp.where(arrives, coming, stays)
    taken = totals.astype(jnp.int32)
    lane = iota((8, LANES), 1)
    for i in range(count):
        moved = lane_pick(rows_ref[i], jnp.broadcast_to(source[i : i + 1], (8, LANES)))
        moved = jnp.where(lane < taken[i : i + 1], moved, 0.0)
        start = jnp.max(starts[i : i + 1]).astype(jnp.int32)
        shift = jnp.bitwise_and(start, LANES - 1)
        block = lax.shift_right_logical(start, 7)
        moved = pltpu.roll(moved, shift, 1)
        packed_ref[block] += jnp.where(lane >= shift, moved, 0.0)
        packed_ref[block + 1] += jnp.where(lane < shift, moved, 0.0)
    return jnp.max(starts[padded - 1 :] + totals[padded - 1 :]).astype(jnp.int32)


def env_scalars(even, odd, harm):
    blocks = [even[64 * i : 64 * i + 64] for i in range(even_count)]
    blocks += [odd[64 * i : 64 * i + 64] for i in range(3)]
    product = {m: blocks[i] * harm[m] for i, m in enumerate(order)}
    return jnp.concatenate(
        [
            product[0],
            product[1] + product[2] + product[3],
            product[4] + product[5] + product[6] + product[7] + product[8],
        ],
        axis=0,
    )


def refined(hidden, ahead, pool, harm, sums, weight_top, weight_rest):
    top, rest = split(pool)
    first = ((0,), (0,))
    width = 64 * even_count
    even = mm(top[:, :width], sums[0], first) + mm(rest[:, :width], sums[0], first)
    odd = mm(top[:, width:], sums[1], first) + mm(rest[:, width:], sums[1], first)
    return hidden + silu(ahead + dot3(weight_top, weight_rest, env_scalars(even, odd, harm)))


def front_kernel(
    layout,
    gathered_ref,
    small_ref,
    halves_ref,
    hidden_ref,
    geo_ref,
    static_ref,
    home_ref,
    env_ref,
    up_ref,
    mid_ref,
    down_ref,
    rows_ref,
    chosen_ref,
    packed_ref,
    pool_ref,
    coming_ref,
    packed_in_ref,
    slots_ref,
    pool_in_ref,
):
    (here_x, here_y), (at_x, at_y) = layout.position()
    home_ref[...] = gathered_ref[layout.at_home(here_x, here_y)]

    def home_of(x, y):
        return layout.at_home(at_x + x, at_y + y)

    tiles, entries, static = look_up(gathered_ref, home_of, (0, 0))
    static_ref[...] = static
    lane = iota((1, LANES), 1)
    first_atom = home_of(0, 0) * ATOMS + 1
    slots = jnp.where(lane < ATOMS, (first_atom + lane).astype(f32), entries[0:1])
    slots = jnp.broadcast_to(slots, (LANES, LANES)).T[: 2 * ATOMS]

    named = [jnp.where(slots[ATOMS:] == tile[5:6], tile[6:7], 0.0) for tile in tiles]
    named = jnp.max(jnp.maximum(*named), axis=1, keepdims=True) > 0
    slots = jnp.concatenate([slots[:ATOMS], jnp.where(named, slots[ATOMS:], -1.0)], axis=0)

    def touches(slots, tile, nearest):
        found = slots == tile[5:6]
        if nearest:
            found = found | (slots == tile[4:5])
        return jnp.max(jnp.where(found, 1.0, 0.0), axis=0, keepdims=True)

    chosen_ref[...] = jnp.zeros_like(chosen_ref)
    domains = near_domains(layout, 2)
    rows = 2 * len(domains) - 2
    rows_in = coming_ref.shape[0]
    for i, offset in enumerate(domains[1:]):
        others, _, _ = look_up(gathered_ref, home_of, offset)
        for half, tile in enumerate(others):
            at = 2 * i + half
            rows_ref[at] = tile
            if at < rows_in:
                place = tile[5:6].astype(jnp.int32) - first_atom
                coming = jnp.where((place >= 0) & (place < ATOMS), tile[6:7], 0.0)
                coming_ref[at : at + 1, :] = coming
    count_in = pack(rows_ref, coming_ref, packed_in_ref, rows_in)
    tiles_in = lax.shift_right_logical(count_in + LANES - 1, 7)

    incoming = packed_in_ref[0]
    slots = jnp.concatenate([slots, jnp.broadcast_to(incoming[4:5], (LANES, LANES)).T], axis=0)

    def choose(slots):
        for at in range(rows):
            tile = rows_ref[at]
            live = tile[6:7] - coming_ref[at : at + 1, :] if at < rows_in else tile[6:7]
            row = slice(at, at + 1)
            found = touches(slots, tile, at < rows_in) * live
            chosen_ref[row, :] = jnp.maximum(chosen_ref[row, :], found)

    choose(slots)

    def add_slots(tile, carry):
        ids = jnp.broadcast_to(packed_in_ref[tile][4:5], (LANES, LANES)).T
        slots_ref[tile] = ids
        choose(ids)
        return carry

    lax.fori_loop(1, tiles_in, add_slots, 0)
    count = pack(rows_ref, chosen_ref, packed_ref, rows)

    def found_in(slots, edges):
        slots = jnp.concatenate([slots] * (edges.shape[1] // LANES), axis=1)
        return [(slots == edges[at : at + 1]).astype(f32) for at in (4, 5)]

    embed = small_ref[small_ref.shape[0] - 1][:64].astype(f32).T.astype(bf16)

    def first_terms(edges):
        units, length, harm = geometry(edges[0:1], edges[1:2], edges[2:3])
        hidden = first_hidden(length, edges[3:4], edges[7:8], embed)
        return (units, harm, hidden, contributions(hidden, small_ref[0], harm, edges[6:7]))

    edges = jnp.concatenate(tiles + [incoming], axis=1)
    units, harm, hidden, terms = first_terms(edges)
    alive = edges[6:7]
    found = found_in(slots, edges)
    pool_ref[...] = scatter(terms, incidence(*found))
    own = 2 * LANES
    geo_ref[...] = jnp.concatenate(
        [value[:, :own] for value in harm + list(units) + [alive]] + [jnp.zeros((3, own), f32)],
        axis=0,
    )

    def start_in(tile, carry):
        pool_in_ref[tile] = scatter(terms, incidence(*found_in(slots_ref[tile], edges)))
        return carry

    lax.fori_loop(1, tiles_in, start_in, 0)

    def add_edges(edges):
        _, _, _, terms = first_terms(edges)
        pool_ref[...] += scatter(terms, incidence(*found_in(slots, edges)))

        def add_in(tile, carry):
            pool_in_ref[tile] += scatter(terms, incidence(*found_in(slots_ref[tile], edges)))
            return carry

        lax.fori_loop(1, tiles_in, add_in, 0)

    def add_tile(tile, carry):
        add_edges(packed_in_ref[tile])
        return carry

    def add_block(block, carry):
        add_edges(jnp.concatenate([packed_ref[4 * block + i] for i in range(4)], axis=1))
        return carry

    lax.fori_loop(1, tiles_in, add_tile, 0)
    lax.fori_loop(0, lax.shift_right_logical(count + 511, 9), add_block, 0)

    slot = iota(found[0].shape, 0)
    edge = iota(found[0].shape, 1)
    at_slot = slot < 2 * ATOMS
    at_centre = jnp.where(
        edge < own,
        jnp.where(at_slot, found[0], 0.0),
        (slot - 2 * ATOMS == edge - own).astype(f32),
    )
    sums = incidence(at_centre, jnp.where(at_slot, found[1], 0.0))
    size = hidden.shape[0]
    ahead = dot3(halves_ref[0][:, :size], halves_ref[1][:, :size], hidden)
    weight = (halves_ref[0][:, size:], halves_ref[1][:, size:])
    hidden = refined(hidden, ahead, pool_ref[...], harm, sums, *weight)
    hidden_ref[...] = hidden[:, :own]
    terms = contributions(hidden, small_ref[1], harm, alive)
    env_ref[...] = scatter(terms, incidence(*[end[:ATOMS] for end in found]))
    own_top, own_rest = split(pool_ref[:ATOMS])
    first = ((0,), (0,))
    middle = 64 * even_count

    def second_in(tile, carry):
        edges = packed_in_ref[tile]
        _, harm, hidden, _ = first_terms(edges)
        at_other = (slots[:ATOMS] == edges[5:6]).astype(f32).astype(bf16)
        other = mm(own_top, at_other, first) + mm(own_rest, at_other, first)
        centre = pool_in_ref[tile].T
        even, odd = (centre[:middle] + other[:middle], centre[middle:] - other[middle:])
        scalars = jnp.concatenate([hidden, env_scalars(even, odd, harm)], axis=0)
        hidden = hidden + silu(dot3(halves_ref[0], halves_ref[1], scalars))
        terms = contributions(hidden, small_ref[1], harm, 1.0)
        env_ref[...] += scatter(terms, (at_other, -at_other))
        return carry

    lax.fori_loop(1, tiles_in, second_in, 0)
    sends = send_columns(static[1:2])
    top, rest = split(env_ref[...])
    store_sides(mm(sends, top, first) + mm(sends, rest, first), up_ref, mid_ref, down_ref)


def ahead_kernel(
    hidden_ref,
    latent_hbm_ref,
    out_hbm_ref,
    ahead_ref,
    sums_top_ref,
    sums_rest_ref,
    out_top_ref,
    out_rest_ref,
    latent_ref,
    out_ref,
    semaphores,
):
    sources = [latent_hbm_ref.at[1], out_hbm_ref]
    latent_copy, out_copy = fetch(sources, [latent_ref, out_ref], semaphores)
    latent_copy.wait()
    size = hidden_ref.shape[0]
    top, rest = split(latent_ref[...].T)
    ahead_ref[...] = dot3(top[:, :size], rest[:, :size], hidden_ref[...])
    sums_top_ref[...] = top[:, size:]
    sums_rest_ref[...] = rest[:, size:]
    out_copy.wait()
    out_top_ref[...], out_rest_ref[...] = split(out_ref[...])


def last_kernel(
    static_ref,
    hidden_in_ref,
    ahead_ref,
    geo_ref,
    env_ref,
    before_ref,
    after_ref,
    from_up_ref,
    from_down_ref,
    weight_top_ref,
    weight_rest_ref,
    out_top_ref,
    out_rest_ref,
    small_ref,
    totals_ref,
    pool,
):
    pool[:ATOMS, :] = env_ref[...]
    load_sides(pool, ATOMS, before_ref, after_ref, from_up_ref, from_down_ref)
    at_centre, at_other = onehots(static_ref[...])
    sums = incidence(at_centre, at_other)
    harm = [geo_ref[m : m + 1] for m in range(9)]
    hidden = hidden_in_ref[...]
    weight = (weight_top_ref[...], weight_rest_ref[...])
    hidden = refined(hidden, ahead_ref[...], pool[...], harm, sums, *weight)
    latent = silu(dot3(out_top_ref[...], out_rest_ref[...], hidden))
    heads = dot_stacked(small_ref[small_ref.shape[0] - 1][64:80], 2, latent)
    alive = geo_ref[12:13]
    energy = 0.5 * heads[0:1] * alive
    push = heads[1:2] * alive
    shares = jnp.concatenate(
        [energy] + [push * geo_ref[9 + i : 10 + i] for i in range(3)] + [jnp.zeros((4, energy.shape[1]), f32)],
        axis=0,
    )
    plus, minus = sums
    last = ((1,), (1,))
    part = iota((8, LANES), 1) // ATOMS == iota((8, LANES), 0)
    rows = []
    for row in range(2):
        at = slice(row * ATOMS, (row + 1) * ATOMS)
        tiled = jnp.concatenate([plus[at], minus[at], minus[at], minus[at]], axis=0)
        spread = jnp.where(part, exact(shares, tiled, last), 0.0)
        rows.append(jnp.sum(spread, axis=0, keepdims=True))
    totals_ref[...] = jnp.broadcast_to(jnp.concatenate(rows, axis=0)[None], totals_ref.shape)


def finish_kernel(layout, gathered_ref, static_ref, energy_ref, forces_ref):
    (at_x, at_y), _ = layout.position()
    own = gathered_ref[layout.at_work(at_x, at_y)][0:1]
    rows = [
        gathered_ref[layout.at_work(at_x + offset_x[k], at_y + offset_y[k])][1:2] for k in range(8)
    ]
    ghosts = pick_rows(jnp.concatenate(rows, axis=0))
    place = iota((LANES, LANES), 1)
    sends = static_ref[1:2].astype(jnp.int32)
    target = iota((LANES, LANES), 0) == place // ATOMS * ATOMS + sends
    ghosts = jnp.concatenate([ghosts] * 8, axis=0)
    total = own + exact(ghosts, target.astype(bf16), ((1,), (1,)))[0:1]
    energy_ref[...] = total[:, :ATOMS]
    for i in range(3):
        forces_ref[i : i + 1, :] = total[:, (i + 1) * ATOMS : (i + 2) * ATOMS]


def call(kernel, outs, scratch, *operands, far=(), limit=16, work=0):
    spaces = [pltpu.HBM if i in far else pltpu.VMEM for i in range(len(operands))]
    return pl.pallas_call(
        kernel,
        out_shape=[out if hasattr(out, "dtype") else jax.ShapeDtypeStruct(out, f32) for out in outs],
        in_specs=[pl.BlockSpec(memory_space=space) for space in spaces],
        out_specs=[pl.BlockSpec(memory_space=pltpu.VMEM) for _ in outs],
        scratch_shapes=scratch,
        cost_estimate=pl.CostEstimate(flops=work << 28, bytes_accessed=1 << 20, transcendentals=0)
        if work
        else None,
        compiler_params=pltpu.CompilerParams(vmem_limit_bytes=limit * 1024 * 1024),
    )(*operands)


def fetched(operands):
    buffers = [pltpu.VMEM(value.shape, value.dtype) for value in operands]
    return buffers + [pltpu.SemaphoreType.DMA((len(operands),))]


def to_all(copies):
    return lax.all_to_all(copies, ("gx", "gy"), 0, 0, tiled=True)


def exchange(layout, sides, step):
    up, mid, down = sides
    axes = ("gx", "gy")
    up = lax.ppermute(up, axes, layout.shift(step, 0))
    down = lax.ppermute(down, axes, layout.shift(-step, 0))
    to_before = jnp.stack([up[0], mid[0], down[0]])
    to_after = jnp.stack([up[2], mid[1], down[2]])
    before = lax.ppermute(to_before, axes, layout.shift(0, step))
    after = lax.ppermute(to_after, axes, layout.shift(0, -step))
    return (before, after, up, down)


def local(
    layout,
    positions,
    species,
    atom_count,
    send_list,
    edges,
    centre_embed,
    neighbour_embed,
    radial_weight,
    env_weight,
    latent_weight,
    out_weight,
    head_weight,
):
    count_edges = edges.shape[2]
    features = out_weight.shape[0]
    rows = 9 * env_weight.shape[1]
    statics = [
        atom_count[None],
        positions,
        species[None],
        jnp.transpose(send_list[0]),
        edges[0],
    ]
    (copies,) = call(
        static_kernel,
        [(layout.count, 8, LANES)],
        fetched(statics),
        *statics,
        far=range(5),
        limit=60,
    )
    layers, channels = env_weight.shape[:2]

    def half(*shape):
        return jax.ShapeDtypeStruct(shape, bf16)

    joined = [radial_weight.T, centre_embed.T, neighbour_embed.T]
    joined += [env_weight.reshape(layers * channels, features), head_weight]
    latent_turned = jnp.transpose(latent_weight, (0, 2, 1))
    weights = [latent_turned[0], jnp.concatenate(joined, axis=0)]
    latent_halves, small = call(
        weights_kernel,
        [half(2, *latent_weight.shape[1:]), half(layers + 1, 2 * channels, features)],
        fetched(weights),
        *weights,
        far=range(2),
        limit=44,
    )
    gathered = to_all(copies)
    sides = [(ATOMS, rows), (3, 4, rows), (2, 4, rows), (3, 4, rows)]
    geo_shape = (16, count_edges)
    hidden_shape = (features, count_edges)
    domains = len(near_domains(layout, 2))
    rows_in = 2 * len(near_domains(layout, 1)) - 2
    padded = -(-(2 * domains - 2) // 8) * 8
    scratch = [
        pltpu.VMEM((2 * domains - 2, 8, LANES), f32),
        pltpu.VMEM((padded, LANES), f32),
        pltpu.VMEM((2 * domains + 4, 8, LANES), f32),
        pltpu.VMEM((2 * ATOMS + LANES, rows), f32),
        pltpu.VMEM((rows_in, LANES), f32),
        pltpu.VMEM((rows_in + 2, 8, LANES), f32),
        pltpu.VMEM((rows_in, LANES, LANES), f32),
        pltpu.VMEM((rows_in, LANES, rows), f32),
    ]
    hidden, geo, mine, home, env, *out = call(
        functools.partial(front_kernel, layout),
        [hidden_shape, geo_shape, (8, LANES), (8, LANES)] + sides,
        scratch,
        gathered,
        small,
        latent_halves,
        limit=44,
    )
    late = [latent_turned, out_weight]
    ahead, sums_top, sums_rest, out_top, out_rest = call(
        ahead_kernel,
        [hidden_shape]
        + [half(features, latent_weight.shape[2] - features)] * 2
        + [half(*out_weight.shape)] * 2,
        fetched([latent_turned[1], out_weight]),
        hidden,
        *late,
        far=(1, 2),
        work=3,
    )
    ghosts = exchange(layout, out, -1)
    pool = [pltpu.VMEM((2 * ATOMS, rows), f32)]
    (totals,) = call(
        last_kernel,
        [(layout.count, 2, LANES)],
        pool,
        mine,
        hidden,
        ahead,
        geo,
        env,
        *ghosts,
        sums_top,
        sums_rest,
        out_top,
        out_rest,
        small,
    )
    totals = to_all(totals)
    energy, forces = call(
        functools.partial(finish_kernel, layout),
        [(1, ATOMS), (3, ATOMS)],
        [],
        totals,
        home,
    )
    return (energy.reshape(-1), forces)


def solution(mesh):
    layout = Layout(mesh.shape["gx"], mesh.shape["gy"])
    placed = (
        P(None, ("gx", "gy")),
        P(("gx", "gy")),
        P(("gx", "gy")),
        P(("gx", "gy"), None, None),
        P(("gx", "gy"), None, None),
        P(),
        P(),
        P(),
        P(),
        P(),
        P(),
        P(),
    )
    return jax.shard_map(
        functools.partial(local, layout),
        mesh=mesh,
        in_specs=placed,
        out_specs=(P(("gx", "gy")), P(None, ("gx", "gy"))),
        check_vma=False,
    )
```
